32 devices in a mesh: dp: 4 (over x, core), ctx: 8 (over z, y).
Axes of the slice: x: 2, y: 2, z: 4, core: 2. Of those that a mesh axis runs over, the one named last changes fastest.
Arguments:
- tile_embed: bfloat16 [4, 8, 512, 1536], P(None, 'ctx', 'dp'), may hold values from -8 to 8
- tile_counts: int32 [4], replicated, may hold values from 1024 to 4096
- w_in: bfloat16 [1536, 768], replicated, may hold values from -1 to 1
- w_qkv: bfloat16 [768, 2304], replicated, may hold values from -1 to 1
- w_out: bfloat16 [768, 768], replicated, may hold values from -0.21875 to 0.21875
Outputs:
- mixed: bfloat16 [4, 4096, 768], P('dp', 'ctx')
The draws below stay inside these ranges and needn't reach their ends.
Inputs may be any that keep to these rules, and one draw needn't show every extreme that they name: The tissue tiles of slide s fill its first tile_counts[s] positions; the rest are padding.
All inputs are finite; a program needn't handle non-finite values.
Results may differ from the reference program's by a relative error of at most 0.017.
Values may be sent and summed in bfloat16 or wider, within the bound.
No kernel may reach another device: no remote copies, remote signals or barrier semaphores. Data moves between devices by JAX's collectives and lax.ppermute only.
A program may use at most 128 MiB of HBM per device.

```python
import math
import jax
import jax.numpy as jnp
from jax import lax

D = 768
E = 1536
HEAD_TOTAL = 12
ROWS_DEV = 512
SLIDES = 4
N_CTX = 8


def draw_tile_embed(key, part):
    value_key = jax.random.fold_in(jax.random.fold_in(key, 11), 0)
    drawn = jnp.clip(jax.random.normal(value_key, (SLIDES, N_CTX, ROWS_DEV, E), jnp.float32), -6.0, 6.0)
    return drawn.astype(jnp.bfloat16)


def draw_w_in(key, part):
    weights = jnp.clip(jax.random.normal(jax.random.fold_in(key, 12), (E, D), jnp.float32), -6.0, 6.0) * (1.0 / E ** 0.5)
    return jnp.clip(weights, -1.0, 1.0).astype(jnp.bfloat16)


def draw_w_qkv(key, part):
    weights = jnp.clip(jax.random.normal(jax.random.fold_in(key, 13), (D, 3 * D), jnp.float32), -6.0, 6.0) * (3.0 / D) ** 0.5
    return jnp.clip(weights, -1.0, 1.0).astype(jnp.bfloat16)


def touch_ends(array, own_key, smallest, high):
    shape = array.shape
    spot = [jax.random.randint(jax.random.fold_in(own_key, axis), (), 0, shape[axis]) for axis in range(len(shape))]
    array = array.at[tuple(spot)].set(smallest)
    longest = shape.index(max(shape))
    spot[longest] = (spot[longest] + 1) % shape[longest]
    return array.at[tuple(spot)].set(high)


def gaussian(own_key, dims, scale, most, kind=jnp.bfloat16):
    return jnp.clip(scale * jax.random.normal(own_key, dims, jnp.float32), -most, most).astype(kind)


def setup_inputs(seed: int = 0) -> dict:
    key_of = jax.random.split(jax.random.key(seed), 6)
    return {
        "tile_embed": draw_tile_embed(jax.random.fold_in(key_of[5], 71), 0),
        "tile_counts": touch_ends(jax.random.randint(key_of[1], (SLIDES,), ROWS_DEV * N_CTX // 4, ROWS_DEV * N_CTX + 1), jax.random.fold_in(key_of[1], 1), ROWS_DEV * N_CTX // 4, ROWS_DEV * N_CTX).astype(jnp.int32),
        "w_in": draw_w_in(jax.random.fold_in(key_of[5], 71), 0),
        "w_qkv": draw_w_qkv(jax.random.fold_in(key_of[5], 71), 0),
        "w_out": gaussian(key_of[4], (D, D), D ** -0.5, 0.21875),
    }


epsilon = 1e-05

def normalize(values):
    average = lax.optimization_barrier(jnp.mean(values, axis=-1, keepdims=True))
    centered = values - average
    variance = lax.optimization_barrier(jnp.mean(centered * centered, axis=-1, keepdims=True))
    return (centered * lax.rsqrt(variance + epsilon)).astype(jnp.bfloat16)

def attend_rows(qkv, is_valid):
    length = qkv.shape[0]
    model_features = qkv.shape[1] // 3
    head_width = model_features // HEAD_TOTAL
    queries = qkv[:, :model_features].reshape(length, HEAD_TOTAL, head_width).astype(jnp.float32)
    key_rows = qkv[:, model_features:2 * model_features].reshape(length, HEAD_TOTAL, head_width).astype(jnp.float32)
    values = qkv[:, 2 * model_features:].reshape(length, HEAD_TOTAL, head_width).astype(jnp.float32)
    scores = jnp.einsum('qhd,khd->qhk', queries, key_rows) * (1.0 / math.sqrt(head_width))
    key_mask = is_valid[None, None, :]
    running_max = lax.optimization_barrier(jnp.max(jnp.where(key_mask, scores, -1e+30), axis=-1))
    weights = jnp.where(key_mask, jnp.exp(scores - running_max[..., None]), 0.0)
    denominator = lax.optimization_barrier(jnp.sum(weights, axis=-1))
    weighted = jnp.einsum('qhk,khd->qhd', weights.astype(jnp.bfloat16).astype(jnp.float32), values)
    return (weighted, running_max, denominator)

def reference(tile_embed, tile_counts, w_in, w_qkv, w_out):
    slide_total, context_count, row_count, embed_width = tile_embed.shape
    sequence_length = context_count * row_count
    model_features = w_out.shape[0]
    head_width = model_features // HEAD_TOTAL
    results = []
    for slide_index in range(slide_total):
        embedded = tile_embed[slide_index].reshape(sequence_length, embed_width)
        hidden = jnp.dot(embedded, w_in, preferred_element_type=jnp.float32).astype(jnp.bfloat16)
        normed = normalize(hidden.astype(jnp.float32))
        qkv = jnp.dot(normed, w_qkv, preferred_element_type=jnp.float32).astype(jnp.bfloat16)
        positions = jnp.arange(sequence_length, dtype=jnp.int32)
        is_valid = positions < tile_counts[slide_index]
        local_accumulator, local_maximum, local_total = lax.map(lambda branch_pair: attend_rows(branch_pair[0], branch_pair[1]), (qkv.reshape(context_count, row_count, 3 * model_features), is_valid.reshape(context_count, row_count)))
        local_accumulator = local_accumulator.reshape(sequence_length, HEAD_TOTAL, head_width)
        local_maximum = local_maximum.reshape(sequence_length, HEAD_TOTAL)
        local_total = local_total.reshape(sequence_length, HEAD_TOTAL)
        dilated_branch = qkv.reshape(row_count, context_count, 3 * model_features).transpose(1, 0, 2)
        dilated_validity = is_valid.reshape(row_count, context_count).T
        dilated_accumulator, dilated_maximum, dilated_total = lax.map(lambda branch_pair: attend_rows(branch_pair[0], branch_pair[1]), (dilated_branch, dilated_validity))
        dilated_output = (dilated_accumulator / dilated_total[..., None]).astype(jnp.bfloat16)
        dilated_output = lax.optimization_barrier(dilated_output).astype(jnp.float32)
        dilated_logsumexp = dilated_maximum + jnp.log(dilated_total)
        dilated_output = dilated_output.transpose(1, 0, 2, 3).reshape(sequence_length, HEAD_TOTAL, head_width)
        dilated_logsumexp = dilated_logsumexp.transpose(1, 0, 2).reshape(sequence_length, HEAD_TOTAL)
        combined_output = jnp.maximum(local_maximum, dilated_logsumexp)
        local_weight = jnp.exp(local_maximum - combined_output)
        dilated_weight = jnp.exp(dilated_logsumexp - combined_output)
        attention_fn = (local_weight[..., None] * local_accumulator + dilated_weight[..., None] * dilated_output) / (local_weight * local_total + dilated_weight)[..., None]
        attention_fn = attention_fn.reshape(sequence_length, model_features).astype(jnp.bfloat16)
        mixed = jnp.dot(attention_fn, w_out, preferred_element_type=jnp.float32)
        mixed = jnp.where(is_valid[:, None], mixed, 0.0).astype(jnp.bfloat16)
        results.append(mixed)
    return jnp.stack(results, axis=0)
```

```python
import functools
import math

import jax
import jax.numpy as jnp
from jax import lax
from jax.experimental import pallas as pl
from jax.experimental.pallas import tpu as pltpu
from jax.sharding import PartitionSpec as P

HEAD_TOTAL = 12
EPSILON = 1e-05
F32 = jnp.float32
BF16 = jnp.bfloat16
NT = (((1,), (1,)), ((), ()))
MIB = 1024 * 1024


def dot(a, b):
    return jnp.dot(a, b, preferred_element_type=F32)


def iota(shape, dim):
    return lax.broadcasted_iota(jnp.int32, shape, dim)


def embed_kernel(ctx, steps, x_ref, w_ref, by_residue_ref, *rest):
    slides, _, sub, width = x_ref.shape
    slide_refs, total = rest[:-1], rest[-1]
    step = pl.program_id(0)
    product = dot(x_ref[...].reshape(slides * sub, width), w_ref[...])

    @pl.when(step == 0)
    def _():
        total[...] = product

    @pl.when(step > 0)
    def _():
        total[...] += product

    @pl.when(step == steps - 1)
    def _():
        me = lax.axis_index("dp")
        each = sub // ctx
        target, source = iota((sub, sub), 0), iota((sub, sub), 1)
        order = (source == target % each * ctx + target // each).astype(BF16)
        for other in range(slides):
            slide = me ^ other
            rows = pl.ds(pl.multiple_of(slide * sub, sub), sub)
            hidden = total[rows, :].astype(BF16).astype(F32)
            centered = hidden - jnp.mean(hidden, axis=-1, keepdims=True)
            variance = jnp.mean(centered * centered, axis=-1, keepdims=True)
            normed = (centered * lax.rsqrt(variance + EPSILON)).astype(BF16)
            sorted_rows = dot(order, normed).astype(BF16)
            slide_refs[other][...] = sorted_rows
            if by_residue_ref is not None:
                by_residue_ref[:, pl.ds(slide, 1)] = sorted_rows.reshape(ctx, 1, each, -1)


def embed(tile_embed, w_in, ctx, split):
    slides, _, sub, width = tile_embed.shape
    features = w_in.shape[1]
    steps = 3
    part = width // steps
    outs = [jax.ShapeDtypeStruct((sub, features), BF16)] * slides
    specs = [pl.BlockSpec((sub, features), lambda i: (0, 0))] * slides
    if split:
        outs = [jax.ShapeDtypeStruct((ctx, slides, sub // ctx, features), BF16)] + outs
        specs = [pl.BlockSpec((ctx, slides, sub // ctx, features), lambda i: (0, 0, 0, 0))] + specs
        body = functools.partial(embed_kernel, ctx, steps)
    else:

        def body(x_ref, w_ref, *rest):
            embed_kernel(ctx, steps, x_ref, w_ref, None, *rest)

    return pl.pallas_call(
        body,
        out_shape=outs,
        grid=(steps,),
        in_specs=[
            pl.BlockSpec((slides, 1, sub, part), lambda i: (0, 0, 0, i)),
            pl.BlockSpec((part, features), lambda i: (i, 0)),
        ],
        out_specs=specs,
        scratch_shapes=[pltpu.VMEM((slides * sub, features), F32)],
        compiler_params=pltpu.CompilerParams(vmem_limit_bytes=24 * MIB),
        name="embed",
    )(tile_embed, w_in)


def project(rows, weight_ref, is_valid, keys, values):
    features = weight_ref.shape[0]
    made = dot(rows, weight_ref[:, features : 2 * features])
    keys[...] = jnp.where(is_valid, made, made[0:1]).astype(BF16)
    made = dot(rows, weight_ref[:, 2 * features :])
    values[...] = jnp.where(is_valid, made, 0.0).astype(BF16)


def queries_of(rows, weight_ref):
    features = weight_ref.shape[0]
    scale = math.log2(math.e) / math.sqrt(features // HEAD_TOTAL)
    return (dot(rows, weight_ref[:, :features]) * scale).astype(BF16)


def attend(queries, keys, values, counted, put, put_total):
    count, features = queries.shape
    width = features // HEAD_TOTAL
    pair = 2 * width
    even = iota((1, pair), 1) < width
    lane = iota((1, 128), 1)
    logs = jnp.zeros((count, 128), F32)
    for at in range(0, features, pair):
        columns = slice(at, at + pair)
        both = queries[:, columns]
        key_pair = keys[:, columns]
        value_pair = jnp.concatenate([values[:, columns], counted], axis=1)
        outs = []
        for side in range(2):
            mine = even if side == 0 else ~even
            scores = lax.dot_general(jnp.where(mine, both, 0).astype(BF16), key_pair, NT, preferred_element_type=F32)
            top = jnp.max(scores, axis=-1, keepdims=True)
            weights = jnp.exp2(scores - top).astype(BF16)
            summed = dot(weights, value_pair)
            outs.append(summed)
            logs = jnp.where(lane == at // width + side, top + jnp.log2(summed[:, pair : pair + 128]), logs)
        total = jnp.where(even, outs[0][:, pair:], outs[1][:, pair:])
        out = jnp.where(even, outs[0][:, :pair], outs[1][:, :pair])
        put(columns, (out / jnp.where(total > 0, total, 1.0)).astype(BF16))
    put_total(logs)


def local_kernel(dp, ctx, block, counts_ref, *refs):
    pieces, (weight_ref, out_ref, log_ref, rows, keys, values) = refs[:dp], refs[dp:]
    me = lax.axis_index("dp")
    sub = pieces[0].shape[0]
    for other, piece in enumerate(pieces):
        rows[pl.ds(pl.multiple_of((me ^ other) * sub, sub), sub), :] = piece[...]
    count = rows.shape[0]
    each = sub // ctx
    spot = iota((count, 1), 0)
    inner = spot % sub
    position = lax.axis_index("ctx") * count + spot // sub * sub + inner % each * ctx + inner // each
    is_valid = position < counts_ref[me]
    project(rows[...], weight_ref, is_valid, keys, values)
    counted = jnp.broadcast_to(is_valid.astype(F32), (count, 128)).astype(BF16)
    for start in range(0, count, block):

        def put(columns, out):
            out_ref[start : start + block, columns] = out

        def put_total(logs):
            log_ref[start : start + block, :] = logs

        attend(queries_of(rows[start : start + block, :], weight_ref), keys, values, counted, put, put_total)


def local_attention(tile_counts, pieces, w_qkv, ctx):
    dp = len(pieces)
    sub, features = pieces[0].shape
    count = dp * sub
    vmem = pl.BlockSpec(memory_space=pltpu.VMEM)
    return pl.pallas_call(
        functools.partial(local_kernel, dp, ctx, min(256, count)),
        out_shape=[jax.ShapeDtypeStruct((count, features), BF16), jax.ShapeDtypeStruct((count, 128), F32)],
        in_specs=[pl.BlockSpec(memory_space=pltpu.SMEM)] + [vmem] * (dp + 1),
        out_specs=[vmem] * 2,
        scratch_shapes=[pltpu.VMEM((count, features), BF16)] * 3,
        compiler_params=pltpu.CompilerParams(vmem_limit_bytes=24 * MIB),
        cost_estimate=pl.CostEstimate(flops=9 * 10**9, bytes_accessed=8 * 10**6, transcendentals=0),
        name="local",
    )(tile_counts, *pieces, w_qkv)


def dilated_kernel(dp, ctx, block, sends, counts_ref, rows_ref, weight_ref, *refs):
    out_refs, (rows, keys, values) = refs[:-3], refs[-3:]
    me, mine = lax.axis_index("dp"), lax.axis_index("ctx")
    count, features = rows_ref.shape
    portion = count // ctx
    each = portion // dp
    spot = iota((count, 1), 0)
    inner = spot % portion
    position = spot // portion * count + inner // each * (count // dp) + inner % each * ctx + mine
    is_valid = position < counts_ref[me]
    project(rows_ref[...], weight_ref, is_valid, keys, values)
    counted = jnp.broadcast_to(is_valid.astype(F32), (count, 128)).astype(BF16)
    if sends is None:
        source = rows_ref
    else:
        source = rows
        for place, other in enumerate(sends):
            at = pl.multiple_of((mine ^ other) * portion, portion)
            rows[place * portion : (place + 1) * portion, :] = rows_ref[pl.ds(at, portion), :]
    for start in range(0, count, block):

        def spread(columns, out):
            for at in range(start, start + block, portion):
                piece = out[at - start : at - start + portion]
                if sends is None:
                    out_refs[0][at : at + portion, columns] = piece
                else:
                    out_refs[at // portion][:, columns] = piece

        def put_total(logs):
            high = logs.astype(BF16).astype(F32)
            low = logs - high
            lane = iota((1, 128), 1)
            both = jnp.where(lane < 16, high, pltpu.roll(low, 16, 1))
            spread(slice(features, features + 128), jnp.where(lane < 32, both, 0.0).astype(BF16))

        attend(queries_of(source[start : start + block, :], weight_ref), keys, values, counted, spread, put_total)


def dilated_attention(tile_counts, rows, w_qkv, dp, ctx, sends):
    count, features = rows.shape
    vmem = pl.BlockSpec(memory_space=pltpu.VMEM)
    if sends is None:
        outs = [jax.ShapeDtypeStruct((count, features + 128), BF16)]
    else:
        outs = [jax.ShapeDtypeStruct((count // ctx, features + 128), BF16)] * ctx
    return pl.pallas_call(
        functools.partial(dilated_kernel, dp, ctx, min(256, count), sends),
        out_shape=outs,
        in_specs=[pl.BlockSpec(memory_space=pltpu.SMEM)] + [vmem] * 2,
        out_specs=[vmem] * len(outs),
        scratch_shapes=[pltpu.VMEM((count, features), BF16)] * 3,
        compiler_params=pltpu.CompilerParams(vmem_limit_bytes=24 * MIB),
        cost_estimate=pl.CostEstimate(flops=9 * 10**9, bytes_accessed=8 * 10**6, transcendentals=0),
        name="dilated",
    )(tile_counts, rows, w_qkv)


def merge_kernel(dp, ctx, sends, counts_ref, out_ref, log_ref, weight_ref, *refs):
    received, (mixed_ref, dilated) = refs[:-2], refs[-2:]
    me, mine = lax.axis_index("dp"), lax.axis_index("ctx")
    count, features = out_ref.shape
    sub = count // dp
    each = sub // ctx
    if sends is None:
        dilated[...] = received[0][...]
    else:
        for other, piece in zip(sends, received):
            for part in range(dp):
                at = pl.multiple_of(part * sub + (mine ^ other) * each, each)
                dilated[pl.ds(at, each), :] = piece[part * each : (part + 1) * each, :]
    lane = iota((1, 128), 1)
    heads = iota((128, features), 0) == iota((128, features), 1) // (features // HEAD_TOTAL)
    heads = heads.astype(BF16)
    target, source = iota((sub, sub), 0), iota((sub, sub), 1)
    order = (target == source % each * ctx + source // each).astype(BF16)
    for part in range(dp):
        rows = slice(part * sub, (part + 1) * sub)
        logs = dilated[rows, features:].astype(F32)
        logs = logs + pltpu.roll(logs, 128 - 16, 1)
        share = jnp.where(lane < HEAD_TOTAL, 1.0 / (1.0 + jnp.exp2(log_ref[rows, :] - logs)), 0.0)
        high = share.astype(BF16)
        low = (share - high.astype(F32)).astype(BF16)
        wide = dot(high, heads) + dot(low, heads)
        own = out_ref[rows, :].astype(F32)
        merged = own + wide * (dilated[rows, :features].astype(F32) - own)
        inner = iota((sub, 1), 0)
        position = mine * count + part * sub + inner % each * ctx + inner // each
        mixed = jnp.where(position < counts_ref[me], dot(merged.astype(BF16), weight_ref[...]), 0.0)
        mixed_ref[0, rows, :] = dot(order, mixed.astype(BF16)).astype(BF16)


def merge(tile_counts, out, logs, w_out, received, dp, ctx, sends):
    count, features = out.shape
    vmem = pl.BlockSpec(memory_space=pltpu.VMEM)
    return pl.pallas_call(
        functools.partial(merge_kernel, dp, ctx, sends),
        out_shape=jax.ShapeDtypeStruct((1, count, features), BF16),
        in_specs=[pl.BlockSpec(memory_space=pltpu.SMEM)] + [vmem] * (3 + len(received)),
        out_specs=vmem,
        scratch_shapes=[pltpu.VMEM((count, features + 128), BF16)],
        compiler_params=pltpu.CompilerParams(vmem_limit_bytes=24 * MIB),
        name="merge",
    )(tile_counts, out, logs, w_out, *received)


def exchange(value, axis, other):
    if other == 0:
        return value
    return lax.ppermute(value, axis, [(i, i ^ other) for i in range(lax.axis_size(axis))])


def body(tile_embed, tile_counts, w_in, w_qkv, w_out):
    dp, ctx = lax.axis_size("dp"), lax.axis_size("ctx")
    slides, _, sub, _ = tile_embed.shape
    features = w_out.shape[0]
    count = sub * dp
    each = sub // ctx
    aligned = each % 16 == 0 and ctx <= 8
    made = embed(tile_embed, w_in, ctx, aligned)
    if aligned:
        by_residue, made = made[0], made[1:]
    else:
        slide_of = [lax.axis_index("dp") ^ other for other in range(dp)]
        stacked = jnp.stack(made)[jnp.stack(slide_of)]
        by_residue = stacked.reshape(slides, ctx, each, features).swapaxes(0, 1)
    regrouped = lax.all_to_all(
        by_residue.reshape(ctx * dp, each, features), ("ctx", "dp"), split_axis=0, concat_axis=0, tiled=True
    ).reshape(count, features)
    pieces = [exchange(piece, "dp", other) for other, piece in enumerate(made)]
    out, logs = local_attention(tile_counts, pieces, w_qkv, ctx)
    if aligned:
        sends = [4, 5, 6, 7, 2, 3, 1, 0] if ctx == 8 else list(range(ctx))
        made = dilated_attention(tile_counts, regrouped, w_qkv, dp, ctx, sends)
        received = [exchange(piece, "ctx", other) for other, piece in zip(sends, made)]
    else:
        sends = None
        made = dilated_attention(tile_counts, regrouped, w_qkv, dp, ctx, sends)[0]
        received = lax.all_to_all(made.reshape(ctx, count // ctx, -1), "ctx", split_axis=0, concat_axis=0, tiled=True)
        received = received.reshape(ctx, dp, each, -1).swapaxes(0, 1).reshape(count, -1)
        received = [received]
    return merge(tile_counts, out, logs, w_out, received, dp, ctx, sends)


def solution(mesh):
    in_specs = (P(None, "ctx", "dp", None), P(), P(), P(), P())
    out_specs = P("dp", "ctx", None)
    return jax.shard_map(body, mesh=mesh, in_specs=in_specs, out_specs=out_specs, check_vma=False)
```

```python
import functools
import math

import jax
import jax.numpy as jnp
from jax import lax
from jax.experimental import pallas as pl
from jax.experimental.pallas import tpu as pltpu
from jax.sharding import PartitionSpec as P

HEAD_TOTAL = 12
EPSILON = 1e-05
F32 = jnp.float32
BF16 = jnp.bfloat16
NT = (((1,), (1,)), ((), ()))
MIB = 1024 * 1024


def dot(a, b):
    return jnp.dot(a, b, preferred_element_type=F32)


def iota(shape, dim):
    return lax.broadcasted_iota(jnp.int32, shape, dim)


def embed_kernel(ctx, steps, split, x_hbm, w_hbm, *refs):
    slides, _, sub, width = x_hbm.shape
    outs = refs[: slides + split]
    x_parts, w_parts, made, arrived, sent = refs[slides + split :]
    part = width // steps
    loads = []
    for step in range(steps):
        columns = pl.ds(step * part, part)
        loads.append(
            (
                pltpu.make_async_copy(w_hbm.at[columns], w_parts.at[step], arrived.at[0, step]),
                pltpu.make_async_copy(x_hbm.at[:, 0, :, columns], x_parts.at[step], arrived.at[1, step]),
            )
        )
        for load in loads[-1]:
            load.start()
    total = None
    for step in range(steps):
        for load in loads[step]:
            load.wait()
        product = dot(x_parts[step].reshape(slides * sub, part), w_parts[step])
        total = product if total is None else total + product
    hidden = total.astype(BF16).astype(F32)
    centered = hidden - jnp.mean(hidden, axis=-1, keepdims=True)
    variance = jnp.mean(centered * centered, axis=-1, keepdims=True)
    normed = (centered * lax.rsqrt(variance + EPSILON)).astype(BF16)
    me = lax.axis_index("dp")
    each = sub // ctx
    target, source = iota((sub, sub), 0), iota((sub, sub), 1)
    order = (source == target % each * ctx + target // each).astype(BF16)
    for slide in range(slides):
        made[slide] = dot(order, normed[slide * sub : (slide + 1) * sub]).astype(BF16).reshape(made.shape[1:])
    stores = []
    if split:
        for slide in range(slides):
            stores.append(pltpu.make_async_copy(made.at[slide], outs[0].at[:, slide], sent.at[1, slide]))
            stores[-1].start()
    for other in range(slides):
        stores.append(pltpu.make_async_copy(made.at[me ^ other], outs[split + other], sent.at[0, other]))
        stores[-1].start()
    for store in stores:
        store.wait()


def embed(tile_embed, w_in, ctx, split):
    slides, _, sub, width = tile_embed.shape
    features = w_in.shape[1]
    steps = 3
    part = width // steps
    shape = (ctx, sub // ctx, features) if split else (sub, features)
    outs = [jax.ShapeDtypeStruct(shape, BF16)] * slides
    if split:
        outs = [jax.ShapeDtypeStruct((ctx, slides, sub // ctx, features), BF16)] + outs
    hbm = pl.BlockSpec(memory_space=pltpu.HBM)
    return pl.pallas_call(
        functools.partial(embed_kernel, ctx, steps, int(split)),
        out_shape=outs,
        in_specs=[hbm] * 2,
        out_specs=[hbm] * len(outs),
        scratch_shapes=[
            pltpu.VMEM((steps, slides, sub, part), BF16),
            pltpu.VMEM((steps, part, features), BF16),
            pltpu.VMEM((slides,) + shape, BF16),
            pltpu.SemaphoreType.DMA((2, steps)),
            pltpu.SemaphoreType.DMA((2, slides)),
        ],
        compiler_params=pltpu.CompilerParams(vmem_limit_bytes=24 * MIB),
        name="embed",
    )(tile_embed, w_in)


def project(rows, weight_ref, is_valid, keys, values):
    features = weight_ref.shape[0]
    made = dot(rows, weight_ref[:, features : 2 * features])
    keys[...] = jnp.where(is_valid, made, made[0:1]).astype(BF16)
    made = dot(rows, weight_ref[:, 2 * features :])
    values[...] = jnp.where(is_valid, made, 0.0).astype(BF16)


def queries_of(rows, weight_ref):
    features = weight_ref.shape[0]
    scale = math.log2(math.e) / math.sqrt(features // HEAD_TOTAL)
    return (dot(rows, weight_ref[:, :features]) * scale).astype(BF16)


def attend(queries, keys, values, counted, put, put_total):
    count, features = queries.shape
    width = features // HEAD_TOTAL
    pair = 2 * width
    even = iota((1, pair), 1) < width
    lane = iota((1, 128), 1)
    logs = jnp.zeros((count, 128), F32)
    for at in range(0, features, pair):
        columns = slice(at, at + pair)
        both = queries[:, columns]
        key_pair = keys[:, columns]
        value_pair = jnp.concatenate([values[:, columns], counted], axis=1)
        outs = []
        for side in range(2):
            mine = even if side == 0 else ~even
            scores = lax.dot_general(jnp.where(mine, both, 0).astype(BF16), key_pair, NT, preferred_element_type=F32)
            top = jnp.max(scores, axis=-1, keepdims=True)
            weights = jnp.exp2(scores - top).astype(BF16)
            summed = dot(weights, value_pair)
            outs.append(summed)
            logs = jnp.where(lane == at // width + side, top + jnp.log2(summed[:, pair : pair + 128]), logs)
        total = jnp.where(even, outs[0][:, pair:], outs[1][:, pair:])
        out = jnp.where(even, outs[0][:, :pair], outs[1][:, :pair])
        put(columns, (out / jnp.where(total > 0, total, 1.0)).astype(BF16))
    put_total(logs)


def local_kernel(dp, ctx, block, counts_ref, *refs):
    pieces, (weight_ref, out_ref, log_ref, rows, keys, values) = refs[:dp], refs[dp:]
    me = lax.axis_index("dp")
    sub = pieces[0].shape[0]
    for other, piece in enumerate(pieces):
        rows[pl.ds(pl.multiple_of((me ^ other) * sub, sub), sub), :] = piece[...]
    count = rows.shape[0]
    each = sub // ctx
    spot = iota((count, 1), 0)
    inner = spot % sub
    position = lax.axis_index("ctx") * count + spot // sub * sub + inner % each * ctx + inner // each
    is_valid = position < counts_ref[me]
    project(rows[...], weight_ref, is_valid, keys, values)
    counted = jnp.broadcast_to(is_valid.astype(F32), (count, 128)).astype(BF16)
    for start in range(0, count, block):

        def put(columns, out):
            out_ref[start : start + block, columns] = out

        def put_total(logs):
            log_ref[start : start + block, :] = logs

        attend(queries_of(rows[start : start + block, :], weight_ref), keys, values, counted, put, put_total)


def local_attention(tile_counts, pieces, w_qkv, ctx):
    dp = len(pieces)
    sub, features = pieces[0].shape
    count = dp * sub
    vmem = pl.BlockSpec(memory_space=pltpu.VMEM)
    return pl.pallas_call(
        functools.partial(local_kernel, dp, ctx, min(256, count)),
        out_shape=[jax.ShapeDtypeStruct((count, features), BF16), jax.ShapeDtypeStruct((count, 128), F32)],
        in_specs=[pl.BlockSpec(memory_space=pltpu.SMEM)] + [vmem] * (dp + 1),
        out_specs=[vmem] * 2,
        scratch_shapes=[pltpu.VMEM((count, features), BF16)] * 3,
        compiler_params=pltpu.CompilerParams(vmem_limit_bytes=24 * MIB),
        cost_estimate=pl.CostEstimate(flops=9 * 10**9, bytes_accessed=8 * 10**6, transcendentals=0),
        name="local",
    )(tile_counts, *pieces, w_qkv)


def packed_rows(portion, features):
    return portion * (features // 128) + 16


def dilated_kernel(dp, ctx, block, sends, counts_ref, rows_hbm, weight_ref, *refs):
    out_refs, (rows, keys, values, ready) = refs[:-4], refs[-4:]
    me, mine = lax.axis_index("dp"), lax.axis_index("ctx")
    count, features = rows_hbm.shape
    portion = count // ctx
    each = portion // dp
    quarter = count // 4
    loads = []
    for part in range(4):
        span = pl.ds(part * quarter, quarter)
        loads.append(pltpu.make_async_copy(rows_hbm.at[span], rows.at[span], ready.at[part]))
        loads[-1].start()
    spot = iota((count, 1), 0)
    inner = spot % portion
    position = spot // portion * count + inner // each * (count // dp) + inner % each * ctx + mine
    is_valid = position < counts_ref[me]
    counted = jnp.broadcast_to(is_valid.astype(F32), (count, 128)).astype(BF16)
    for load in loads:
        load.wait()
    project(rows[...], weight_ref, is_valid, keys, values)
    portions = block // portion
    for start in range(0, len(sends), portions):
        some = sends[start : start + portions]
        wanted = []
        for other in some:
            at = pl.multiple_of((mine ^ other) * portion, portion)
            wanted.append(rows[pl.ds(at, portion), :])

        def spread(columns, out):
            for place in range(len(some)):
                first = columns.start // 128 * portion
                out_refs[start + place][first : first + portion, :] = out[place * portion : (place + 1) * portion]

        def put_total(logs):
            high = logs.astype(BF16).astype(F32)
            low = logs - high
            lane = iota((1, 128), 1)
            both = jnp.where(lane < 16, high, pltpu.roll(low, 16, 1))
            both = jnp.where(lane < 32, both, 0.0)
            for place in range(len(some)):
                merged = both[place * portion : place * portion + 16]
                for group in range(1, portion // 16):
                    at = place * portion + group * 16
                    merged = merged + pltpu.roll(both[at : at + 16], 32 * group, 1)
                out_refs[start + place][-16:, :] = merged.astype(BF16)

        attend(queries_of(jnp.concatenate(wanted, axis=0), weight_ref), keys, values, counted, spread, put_total)


def dilated_attention(tile_counts, rows, w_qkv, dp, ctx, sends):
    count, features = rows.shape
    portion = count // ctx
    vmem = pl.BlockSpec(memory_space=pltpu.VMEM)
    outs = [jax.ShapeDtypeStruct((packed_rows(portion, features), 128), BF16)] * len(sends)
    return pl.pallas_call(
        functools.partial(dilated_kernel, dp, ctx, min(256, count), sends),
        out_shape=outs,
        in_specs=[pl.BlockSpec(memory_space=pltpu.SMEM), pl.BlockSpec(memory_space=pltpu.HBM), vmem],
        out_specs=[vmem] * len(outs),
        scratch_shapes=[pltpu.VMEM((count, features), BF16)] * 3 + [pltpu.SemaphoreType.DMA((4,))],
        compiler_params=pltpu.CompilerParams(vmem_limit_bytes=24 * MIB),
        cost_estimate=pl.CostEstimate(flops=6 * 10**9, bytes_accessed=5 * 10**6, transcendentals=0),
        name="dilated",
    )(tile_counts, rows, w_qkv)


def merge_kernel(dp, ctx, sends, counts_ref, out_ref, log_ref, weight_ref, *refs):
    received, (mixed_ref, dilated) = refs[:-2], refs[-2:]
    me, mine = lax.axis_index("dp"), lax.axis_index("ctx")
    count, features = out_ref.shape
    sub = count // dp
    each = sub // ctx
    if sends is None:
        dilated[...] = received[0][...]
    else:
        portion = count // ctx
        for other, piece in zip(sends, received):
            for part in range(dp):
                at = pl.multiple_of(part * sub + (mine ^ other) * each, each)
                for block in range(features // 128):
                    first = block * portion + part * each
                    dilated[pl.ds(at, each), block * 128 : (block + 1) * 128] = piece[first : first + each, :]
                dilated[pl.ds(at, each), features:] = pltpu.roll(
                    piece[-16:, :].astype(F32), (128 - 32 * part) % 128, 1
                ).astype(BF16)
    lane = iota((1, 128), 1)
    heads = iota((128, features), 0) == iota((128, features), 1) // (features // HEAD_TOTAL)
    heads = heads.astype(BF16)
    target, source = iota((sub, sub), 0), iota((sub, sub), 1)
    order = (target == source % each * ctx + source // each).astype(BF16)
    for part in range(dp):
        rows = slice(part * sub, (part + 1) * sub)
        logs = dilated[rows, features:].astype(F32)
        logs = logs + pltpu.roll(logs, 128 - 16, 1)
        share = jnp.where(lane < HEAD_TOTAL, 1.0 / (1.0 + jnp.exp2(log_ref[rows, :] - logs)), 0.0)
        high = share.astype(BF16)
        low = (share - high.astype(F32)).astype(BF16)
        wide = dot(high, heads) + dot(low, heads)
        own = out_ref[rows, :].astype(F32)
        merged = own + wide * (dilated[rows, :features].astype(F32) - own)
        inner = iota((sub, 1), 0)
        position = mine * count + part * sub + inner % each * ctx + inner // each
        mixed = jnp.where(position < counts_ref[me], dot(merged.astype(BF16), weight_ref[...]), 0.0)
        mixed_ref[0, rows, :] = dot(order, mixed.astype(BF16)).astype(BF16)


def merge(tile_counts, out, logs, w_out, received, dp, ctx, sends):
    count, features = out.shape
    vmem = pl.BlockSpec(memory_space=pltpu.VMEM)
    return pl.pallas_call(
        functools.partial(merge_kernel, dp, ctx, sends),
        out_shape=jax.ShapeDtypeStruct((1, count, features), BF16),
        in_specs=[pl.BlockSpec(memory_space=pltpu.SMEM)] + [vmem] * (3 + len(received)),
        out_specs=vmem,
        scratch_shapes=[pltpu.VMEM((count, features + 128), BF16)],
        compiler_params=pltpu.CompilerParams(vmem_limit_bytes=24 * MIB),
        name="merge",
    )(tile_counts, out, logs, w_out, *received)


def exchange(value, axis, other):
    if other == 0:
        return value
    return lax.ppermute(value, axis, [(i, i ^ other) for i in range(lax.axis_size(axis))])


def body(tile_embed, tile_counts, w_in, w_qkv, w_out):
    dp, ctx = lax.axis_size("dp"), lax.axis_size("ctx")
    slides, _, sub, _ = tile_embed.shape
    features = w_out.shape[0]
    count = sub * dp
    each = sub // ctx
    aligned = each % 16 == 0 and ctx <= 8
    made = embed(tile_embed, w_in, ctx, aligned)
    if aligned:
        by_residue, made = made[0], made[1:]
    else:
        slide_of = [lax.axis_index("dp") ^ other for other in range(dp)]
        stacked = jnp.stack(made)[jnp.stack(slide_of)]
        by_residue = stacked.reshape(slides, ctx, each, features).swapaxes(0, 1)
    regrouped = lax.all_to_all(
        by_residue.reshape(ctx * dp, each, features), ("ctx", "dp"), split_axis=0, concat_axis=0, tiled=True
    ).reshape(count, features)
    pieces = [exchange(piece, "dp", other).reshape(sub, features) for other, piece in enumerate(made)]
    out, logs = local_attention(tile_counts, pieces, w_qkv, ctx)
    regrouped, out, logs = lax.optimization_barrier((regrouped, out, logs))
    portion = count // ctx
    if aligned:
        sends, received = [], []
        for some in ([4, 5, 6, 7], [2, 3, 1, 0]) if ctx == 8 else (list(range(ctx)),):
            made = dilated_attention(tile_counts, regrouped, w_qkv, dp, ctx, some)
            received += [exchange(piece, "ctx", other) for other, piece in zip(some, made)]
            sends += some
    else:
        made = dilated_attention(tile_counts, regrouped, w_qkv, dp, ctx, list(range(ctx)))
        order = jnp.stack([lax.axis_index("ctx") ^ other for other in range(ctx)])
        packed = lax.all_to_all(jnp.stack(made)[order], "ctx", split_axis=0, concat_axis=0, tiled=True)
        wide = packed[:, :-16].reshape(ctx, features // 128, portion, 128).swapaxes(1, 2).reshape(ctx, portion, features)
        lanes = packed[:, -16:].reshape(ctx, 16, 4, 32).swapaxes(1, 2)[:, : portion // 16].reshape(ctx, portion, 32)
        whole = jnp.concatenate([wide, jnp.pad(lanes, ((0, 0), (0, 0), (0, 96)))], axis=-1)
        received = [whole.reshape(ctx, dp, each, -1).swapaxes(0, 1).reshape(count, -1)]
        sends = None
    return merge(tile_counts, out, logs, w_out, received, dp, ctx, sends)


def solution(mesh):
    in_specs = (P(None, "ctx", "dp", None), P(), P(), P(), P())
    out_specs = P("dp", "ctx", None)
    return jax.shard_map(body, mesh=mesh, in_specs=in_specs, out_specs=out_specs, check_vma=False)
```

```python
import functools
import math

import jax
import jax.numpy as jnp
from jax import lax
from jax.experimental import pallas as pl
from jax.experimental.pallas import tpu as pltpu
from jax.sharding import PartitionSpec as P

HEAD_TOTAL = 12
EPSILON = 1e-05
F32 = jnp.float32
BF16 = jnp.bfloat16
NT = (((1,), (1,)), ((), ()))
MIB = 1024 * 1024


def dot(a, b):
    return jnp.dot(a, b, preferred_element_type=F32)


def iota(shape, dim):
    return lax.broadcasted_iota(jnp.int32, shape, dim)


def embed_kernel(ctx, steps, split, x_hbm, w_hbm, *refs):
    slides, _, sub, width = x_hbm.shape
    outs = refs[: slides + split]
    x_parts, w_parts, made, arrived, sent = refs[slides + split :]
    part = width // steps
    loads = []
    for step in range(steps):
        columns = pl.ds(step * part, part)
        loads.append(
            (
                pltpu.make_async_copy(w_hbm.at[columns], w_parts.at[step], arrived.at[0, step]),
                pltpu.make_async_copy(x_hbm.at[:, 0, :, columns], x_parts.at[step], arrived.at[1, step]),
            )
        )
        for load in loads[-1]:
            load.start()
    total = None
    for step in range(steps):
        for load in loads[step]:
            load.wait()
        product = dot(x_parts[step].reshape(slides * sub, part), w_parts[step])
        total = product if total is None else total + product
    me = lax.axis_index("dp")
    each = sub // ctx
    target, source = iota((sub, sub), 0), iota((sub, sub), 1)
    order = (source == target % each * ctx + target // each).astype(BF16)
    stores = []
    for slide in range(slides):
        hidden = total[slide * sub : (slide + 1) * sub].astype(BF16).astype(F32)
        centered = hidden - jnp.mean(hidden, axis=-1, keepdims=True)
        variance = jnp.mean(centered * centered, axis=-1, keepdims=True)
        normed = (centered * lax.rsqrt(variance + EPSILON)).astype(BF16)
        made[slide] = dot(order, normed).astype(BF16).reshape(made.shape[1:])
        if split:
            stores.append(pltpu.make_async_copy(made.at[slide], outs[0].at[:, slide], sent.at[1, slide]))
            stores[-1].start()
    for other in range(slides):
        stores.append(pltpu.make_async_copy(made.at[me ^ other], outs[split + other], sent.at[0, other]))
        stores[-1].start()
    for store in stores:
        store.wait()


def embed(tile_embed, w_in, ctx, split):
    slides, _, sub, width = tile_embed.shape
    features = w_in.shape[1]
    steps = 6
    part = width // steps
    shape = (ctx, sub // ctx, features) if split else (sub, features)
    outs = [jax.ShapeDtypeStruct(shape, BF16)] * slides
    if split:
        outs = [jax.ShapeDtypeStruct((ctx, slides, sub // ctx, features), BF16)] + outs
    hbm = pl.BlockSpec(memory_space=pltpu.HBM)
    return pl.pallas_call(
        functools.partial(embed_kernel, ctx, steps, int(split)),
        out_shape=outs,
        in_specs=[hbm] * 2,
        out_specs=[hbm] * len(outs),
        scratch_shapes=[
            pltpu.VMEM((steps, slides, sub, part), BF16),
            pltpu.VMEM((steps, part, features), BF16),
            pltpu.VMEM((slides,) + shape, BF16),
            pltpu.SemaphoreType.DMA((2, steps)),
            pltpu.SemaphoreType.DMA((2, slides)),
        ],
        compiler_params=pltpu.CompilerParams(vmem_limit_bytes=60 * MIB),
        name="embed",
    )(tile_embed, w_in)


def fetch_kernel(source, after, kept, ready):
    copy = pltpu.make_async_copy(source, kept, ready)
    copy.start()
    copy.wait()


def fetch(value, after):
    hbm = pl.BlockSpec(memory_space=pltpu.HBM)
    return pl.pallas_call(
        fetch_kernel,
        out_shape=jax.ShapeDtypeStruct(value.shape, value.dtype),
        in_specs=[hbm] * 2,
        out_specs=pl.BlockSpec(memory_space=pltpu.VMEM),
        scratch_shapes=[pltpu.SemaphoreType.DMA],
        compiler_params=pltpu.CompilerParams(vmem_limit_bytes=50 * MIB),
        cost_estimate=pl.CostEstimate(flops=0, bytes_accessed=8 * 10**6, transcendentals=0),
        name="fetch",
    )(value, after)


def project(rows, weight_ref, is_valid, keys, values):
    features = weight_ref.shape[0]
    made = dot(rows, weight_ref[:, features : 2 * features])
    keys[...] = jnp.where(is_valid, made, made[0:1]).astype(BF16)
    made = dot(rows, weight_ref[:, 2 * features :])
    values[...] = jnp.where(is_valid, made, 0.0).astype(BF16)


def queries_of(rows, weight_ref):
    features = weight_ref.shape[0]
    scale = math.log2(math.e) / math.sqrt(features // HEAD_TOTAL)
    return (dot(rows, weight_ref[:, :features]) * scale).astype(BF16)


def attend(queries, keys, values, counted, put, put_total):
    count, features = queries.shape
    width = features // HEAD_TOTAL
    pair = 2 * width
    even = iota((1, pair), 1) < width
    lane = iota((1, 128), 1)
    logs = jnp.zeros((count, 128), F32)
    for at in range(0, features, pair):
        columns = slice(at, at + pair)
        both = queries[:, columns]
        key_pair = keys[:, columns]
        value_pair = jnp.concatenate([values[:, columns], counted], axis=1)
        outs = []
        for side in range(2):
            mine = even if side == 0 else ~even
            scores = lax.dot_general(jnp.where(mine, both, 0).astype(BF16), key_pair, NT, preferred_element_type=F32)
            top = jnp.max(scores, axis=-1, keepdims=True)
            weights = jnp.exp2(scores - top).astype(BF16)
            summed = dot(weights, value_pair)
            outs.append(summed)
            logs = jnp.where(lane == at // width + side, top + jnp.log2(summed[:, pair : pair + 128]), logs)
        total = jnp.where(even, outs[0][:, pair:], outs[1][:, pair:])
        out = jnp.where(even, outs[0][:, :pair], outs[1][:, :pair])
        put(columns, (out / jnp.where(total > 0, total, 1.0)).astype(BF16))
    put_total(logs)


def local_kernel(dp, ctx, block, counts_ref, *refs):
    pieces, (weight_ref, out_ref, log_ref, rows, keys, values) = refs[:dp], refs[dp:]
    me = lax.axis_index("dp")
    sub = pieces[0].shape[0]
    for other, piece in enumerate(pieces):
        rows[pl.ds(pl.multiple_of((me ^ other) * sub, sub), sub), :] = piece[...]
    count = rows.shape[0]
    each = sub // ctx
    spot = iota((count, 1), 0)
    inner = spot % sub
    position = lax.axis_index("ctx") * count + spot // sub * sub + inner % each * ctx + inner // each
    is_valid = position < counts_ref[me]
    project(rows[...], weight_ref, is_valid, keys, values)
    counted = jnp.broadcast_to(is_valid.astype(F32), (count, 128)).astype(BF16)
    for start in range(0, count, block):

        def put(columns, out):
            out_ref[start : start + block, columns] = out

        def put_total(logs):
            log_ref[start : start + block, :] = logs

        attend(queries_of(rows[start : start + block, :], weight_ref), keys, values, counted, put, put_total)


def local_attention(tile_counts, pieces, w_qkv, ctx):
    dp = len(pieces)
    sub, features = pieces[0].shape
    count = dp * sub
    vmem = pl.BlockSpec(memory_space=pltpu.VMEM)
    return pl.pallas_call(
        functools.partial(local_kernel, dp, ctx, min(256, count)),
        out_shape=[jax.ShapeDtypeStruct((count, features), BF16), jax.ShapeDtypeStruct((count, 128), F32)],
        in_specs=[pl.BlockSpec(memory_space=pltpu.SMEM)] + [vmem] * (dp + 1),
        out_specs=[vmem] * 2,
        scratch_shapes=[pltpu.VMEM((count, features), BF16)] * 3,
        compiler_params=pltpu.CompilerParams(vmem_limit_bytes=24 * MIB),
        cost_estimate=pl.CostEstimate(flops=10**12, bytes_accessed=10**10, transcendentals=0),
        name="local",
    )(tile_counts, *pieces, w_qkv)


def packed_rows(portion, features):
    return portion * (features // 128) + 16


def dilated_kernel(dp, ctx, block, sends, first_call, counts_ref, rows, weight_ref, *refs):
    if first_call:
        out_refs, (keys, values) = refs[:-2], refs[-2:]
    else:
        (keys, values), out_refs = refs[:2], refs[2:]
    me, mine = lax.axis_index("dp"), lax.axis_index("ctx")
    count, features = rows.shape
    portion = count // ctx
    each = portion // dp
    spot = iota((count, 1), 0)
    inner = spot % portion
    position = spot // portion * count + inner // each * (count // dp) + inner % each * ctx + mine
    is_valid = position < counts_ref[me]
    counted = jnp.broadcast_to(is_valid.astype(F32), (count, 128)).astype(BF16)
    if first_call:
        project(rows[...], weight_ref, is_valid, keys, values)
    portions = block // portion
    for start in range(0, len(sends), portions):
        some = sends[start : start + portions]
        wanted = []
        for other in some:
            at = pl.multiple_of((mine ^ other) * portion, portion)
            wanted.append(rows[pl.ds(at, portion), :])

        def spread(columns, out):
            for place in range(len(some)):
                first = columns.start // 128 * portion
                out_refs[start + place][first : first + portion, :] = out[place * portion : (place + 1) * portion]

        def put_total(logs):
            high = logs.astype(BF16).astype(F32)
            low = logs - high
            lane = iota((1, 128), 1)
            both = jnp.where(lane < 16, high, pltpu.roll(low, 16, 1))
            both = jnp.where(lane < 32, both, 0.0)
            for place in range(len(some)):
                merged = both[place * portion : place * portion + 16]
                for group in range(1, portion // 16):
                    at = place * portion + group * 16
                    merged = merged + pltpu.roll(both[at : at + 16], 32 * group, 1)
                out_refs[start + place][-16:, :] = merged.astype(BF16)

        attend(queries_of(jnp.concatenate(wanted, axis=0), weight_ref), keys, values, counted, spread, put_total)


def dilated_attention(tile_counts, rows, w_qkv, dp, ctx, sends, kept=()):
    count, features = rows.shape
    portion = count // ctx
    vmem = pl.BlockSpec(memory_space=pltpu.VMEM)
    outs = [jax.ShapeDtypeStruct((packed_rows(portion, features), 128), BF16)] * len(sends)
    if not kept:
        outs += [jax.ShapeDtypeStruct((count, features), BF16)] * 2
    return pl.pallas_call(
        functools.partial(dilated_kernel, dp, ctx, min(256, count), sends, not kept),
        out_shape=outs,
        in_specs=[pl.BlockSpec(memory_space=pltpu.SMEM)] + [vmem] * (2 + len(kept)),
        out_specs=[vmem] * len(outs),
        compiler_params=pltpu.CompilerParams(vmem_limit_bytes=24 * MIB),
        cost_estimate=pl.CostEstimate(flops=10**6, bytes_accessed=10**4, transcendentals=0),
        name="dilated",
    )(tile_counts, rows, w_qkv, *kept)


def merge_rows(own, own_logs, features_of, logs, heads, weight):
    lane = iota((1, 128), 1)
    share = jnp.where(lane < HEAD_TOTAL, 1.0 / (1.0 + jnp.exp2(own_logs - logs)), 0.0)
    high = share.astype(BF16)
    low = (share - high.astype(F32)).astype(BF16)
    wide = dot(high, heads) + dot(low, heads)
    own = own.astype(F32)
    merged = own + wide * (features_of.astype(F32) - own)
    return dot(merged.astype(BF16), weight)


def heads_of(features):
    return (iota((128, features), 0) == iota((128, features), 1) // (features // HEAD_TOTAL)).astype(BF16)


def merge_kernel(dp, ctx, counts_ref, out_ref, log_ref, weight_ref, dilated, mixed_ref):
    me, mine = lax.axis_index("dp"), lax.axis_index("ctx")
    count, features = out_ref.shape
    sub = count // dp
    each = sub // ctx
    heads = heads_of(features)
    target, source = iota((sub, sub), 0), iota((sub, sub), 1)
    order = (target == source % each * ctx + source // each).astype(BF16)
    for part in range(dp):
        rows = slice(part * sub, (part + 1) * sub)
        logs = dilated[rows, features:].astype(F32)
        logs = logs + pltpu.roll(logs, 128 - 16, 1)
        mixed = merge_rows(out_ref[rows, :], log_ref[rows, :], dilated[rows, :features], logs, heads, weight_ref[...])
        inner = iota((sub, 1), 0)
        position = mine * count + part * sub + inner % each * ctx + inner // each
        mixed = jnp.where(position < counts_ref[me], mixed, 0.0)
        mixed_ref[0, rows, :] = dot(order, mixed.astype(BF16)).astype(BF16)


def merge(tile_counts, out, logs, w_out, received, dp, ctx):
    count, features = out.shape
    vmem = pl.BlockSpec(memory_space=pltpu.VMEM)
    return pl.pallas_call(
        functools.partial(merge_kernel, dp, ctx),
        out_shape=jax.ShapeDtypeStruct((1, count, features), BF16),
        in_specs=[pl.BlockSpec(memory_space=pltpu.SMEM)] + [vmem] * 4,
        out_specs=vmem,
        compiler_params=pltpu.CompilerParams(vmem_limit_bytes=24 * MIB),
        name="merge",
    )(tile_counts, out, logs, w_out, received)


def merge_part_kernel(dp, ctx, sends, with_others, counts_ref, out_ref, log_ref, weight_ref, *refs):
    pieces, refs = refs[: len(sends)], refs[len(sends) :]
    mixed_ref, (dilated, own, own_logs) = refs[-4], refs[-3:]
    me, mine = lax.axis_index("dp"), lax.axis_index("ctx")
    count, features = out_ref.shape
    sub = count // dp
    each = sub // ctx
    portion = count // ctx
    span = len(sends) * each
    first = (mine ^ sends[0]) // len(sends) * len(sends)
    for part in range(dp):
        at = pl.multiple_of(part * sub + first * each, each)
        own[part * span : (part + 1) * span, :] = out_ref[pl.ds(at, span), :]
        own_logs[part * span : (part + 1) * span, :] = log_ref[pl.ds(at, span), :]
    for other, piece in zip(sends, pieces):
        for part in range(dp):
            at = pl.multiple_of(part * span + ((mine ^ other) - first) * each, each)
            for block in range(features // 128):
                start = block * portion + part * each
                dilated[pl.ds(at, each), block * 128 : (block + 1) * 128] = piece[start : start + each, :]
            dilated[pl.ds(at, each), features:] = pltpu.roll(
                piece[-16:, :].astype(F32), (128 - 32 * part) % 128, 1
            ).astype(BF16)
    logs = dilated[:, features:].astype(F32)
    logs = logs + pltpu.roll(logs, 128 - 16, 1)
    mixed = merge_rows(own[...], own_logs[...], dilated[:, :features], logs, heads_of(features), weight_ref[...])
    spot = iota((dp * span, 1), 0)
    inner = spot % span
    position = mine * count + spot // span * sub + inner % each * ctx + first + inner // each
    mixed = jnp.where(position < counts_ref[me], mixed, 0.0).astype(BF16)
    target, source = iota((sub, span), 0), iota((sub, span), 1)
    order = (target == source % each * ctx + first + source // each).astype(BF16)
    for part in range(dp):
        made = dot(order, mixed[part * span : (part + 1) * span])
        rows = slice(part * sub, (part + 1) * sub)
        if with_others:
            made = made + refs[0][rows, :].astype(F32)
            mixed_ref[0, rows, :] = made.astype(BF16)
        else:
            mixed_ref[rows, :] = made.astype(BF16)


def merge_part(tile_counts, out, logs, w_out, received, dp, ctx, sends, others=()):
    count, features = out.shape
    vmem = pl.BlockSpec(memory_space=pltpu.VMEM)
    shape = (1, count, features) if others else (count, features)
    rows = count * len(sends) // ctx
    return pl.pallas_call(
        functools.partial(merge_part_kernel, dp, ctx, sends, len(others)),
        out_shape=jax.ShapeDtypeStruct(shape, BF16),
        in_specs=[pl.BlockSpec(memory_space=pltpu.SMEM)] + [vmem] * (3 + len(received) + len(others)),
        out_specs=vmem,
        scratch_shapes=[
            pltpu.VMEM((rows, features + 128), BF16),
            pltpu.VMEM((rows, features), BF16),
            pltpu.VMEM((rows, 128), F32),
        ],
        compiler_params=pltpu.CompilerParams(vmem_limit_bytes=24 * MIB),
        cost_estimate=pl.CostEstimate(flops=10**6, bytes_accessed=10**4, transcendentals=0),
        name="merge",
    )(tile_counts, out, logs, w_out, *received, *others)


def exchange(value, axis, other):
    if other == 0:
        return value
    return lax.ppermute(value, axis, [(i, i ^ other) for i in range(lax.axis_size(axis))])


def body(tile_embed, tile_counts, w_in, w_qkv, w_out):
    dp, ctx = lax.axis_size("dp"), lax.axis_size("ctx")
    slides, _, sub, _ = tile_embed.shape
    features = w_out.shape[0]
    count = sub * dp
    each = sub // ctx
    aligned = each % 16 == 0 and ctx <= 8
    made = embed(tile_embed, w_in, ctx, aligned)
    if aligned:
        by_residue, made = made[0], made[1:]
    else:
        slide_of = [lax.axis_index("dp") ^ other for other in range(dp)]
        stacked = jnp.stack(made)[jnp.stack(slide_of)]
        by_residue = stacked.reshape(slides, ctx, each, features).swapaxes(0, 1)
    pieces = [exchange(piece, "dp", other).reshape(sub, features) for other, piece in enumerate(made)]
    regrouped = lax.all_to_all(
        by_residue.reshape(ctx * dp, each, features), ("ctx", "dp"), split_axis=0, concat_axis=0, tiled=True
    ).reshape(count, features)
    w_near = fetch(w_qkv, made[0])
    out, logs = local_attention(tile_counts, pieces, w_near, ctx)
    regrouped, out, logs = lax.optimization_barrier((regrouped, out, logs))
    portion = count // ctx
    if aligned:
        found, kept, mixed = {}, (), ()
        halves = ((4, 5, 6, 7), (2, 3, 1, 0)) if ctx == 8 else (tuple(range(ctx)),)
        for some in halves:
            made = dilated_attention(tile_counts, regrouped, w_near, dp, ctx, some, kept)
            made, kept = made[: len(some)], kept or made[len(some) :]
            found.update((other, exchange(piece, "ctx", other)) for other, piece in zip(some, made))
        for some in halves:
            received = [found[other] for other in some]
            mixed = (merge_part(tile_counts, out, logs, w_out, received, dp, ctx, some, mixed),)
        return mixed[0].reshape(1, count, features)
    else:
        made = dilated_attention(tile_counts, regrouped, w_near, dp, ctx, list(range(ctx)))[:ctx]
        order = jnp.stack([lax.axis_index("ctx") ^ other for other in range(ctx)])
        packed = lax.all_to_all(jnp.stack(made)[order], "ctx", split_axis=0, concat_axis=0, tiled=True)
        wide = packed[:, :-16].reshape(ctx, features // 128, portion, 128).swapaxes(1, 2).reshape(ctx, portion, features)
        lanes = packed[:, -16:].reshape(ctx, 16, 4, 32).swapaxes(1, 2)[:, : portion // 16].reshape(ctx, portion, 32)
        whole = jnp.concatenate([wide, jnp.pad(lanes, ((0, 0), (0, 0), (0, 96)))], axis=-1)
        received = whole.reshape(ctx, dp, each, -1).swapaxes(0, 1).reshape(count, -1)
        return merge(tile_counts, out, logs, w_out, received, dp, ctx)


def solution(mesh):
    in_specs = (P(None, "ctx", "dp", None), P(), P(), P(), P())
    out_specs = P("dp", "ctx", None)
    return jax.shard_map(body, mesh=mesh, in_specs=in_specs, out_specs=out_specs, check_vma=False)
```

```python
import functools
import math

import jax
import jax.numpy as jnp
from jax import lax
from jax.experimental import pallas as pl
from jax.experimental.pallas import tpu as pltpu
from jax.sharding import PartitionSpec as P

HEAD_TOTAL = 12
EPSILON = 1e-05
F32 = jnp.float32
BF16 = jnp.bfloat16
NT = (((1,), (1,)), ((), ()))
MIB = 1024 * 1024


def dot(a, b):
    return jnp.dot(a, b, preferred_element_type=F32)


def iota(shape, dim):
    return lax.broadcasted_iota(jnp.int32, shape, dim)


def embed_kernel(ctx, steps, split, x_hbm, w_hbm, *refs):
    slides, _, sub, width = x_hbm.shape
    outs = refs[: slides + split]
    x_parts, w_parts, made, arrived, sent = refs[slides + split :]
    part = width // steps
    loads = []
    for step in range(steps):
        columns = pl.ds(step * part, part)
        loads.append(
            (
                pltpu.make_async_copy(w_hbm.at[columns], w_parts.at[step], arrived.at[0, step]),
                pltpu.make_async_copy(x_hbm.at[:, 0, :, columns], x_parts.at[step], arrived.at[1, step]),
            )
        )
        for load in loads[-1]:
            load.start()
    total = None
    for step in range(steps):
        for load in loads[step]:
            load.wait()
        product = dot(x_parts[step].reshape(slides * sub, part), w_parts[step])
        total = product if total is None else total + product
    me = lax.axis_index("dp")
    each = sub // ctx
    target, source = iota((sub, sub), 0), iota((sub, sub), 1)
    order = (source == target % each * ctx + target // each).astype(BF16)
    stores = []
    for slide in range(slides):
        hidden = total[slide * sub : (slide + 1) * sub].astype(BF16).astype(F32)
        centered = hidden - jnp.mean(hidden, axis=-1, keepdims=True)
        variance = jnp.mean(centered * centered, axis=-1, keepdims=True)
        normed = (centered * lax.rsqrt(variance + EPSILON)).astype(BF16)
        made[slide] = dot(order, normed).astype(BF16).reshape(made.shape[1:])
        if split:
            stores.append(pltpu.make_async_copy(made.at[slide], outs[0].at[:, slide], sent.at[1, slide]))
            stores[-1].start()
    for other in range(slides):
        stores.append(pltpu.make_async_copy(made.at[me ^ other], outs[split + other], sent.at[0, other]))
        stores[-1].start()
    for store in stores:
        store.wait()


def embed(tile_embed, w_in, ctx, split):
    slides, _, sub, width = tile_embed.shape
    features = w_in.shape[1]
    steps = 6
    part = width // steps
    shape = (ctx, sub // ctx, features) if split else (sub, features)
    outs = [jax.ShapeDtypeStruct(shape, BF16)] * slides
    if split:
        outs = [jax.ShapeDtypeStruct((ctx, slides, sub // ctx, features), BF16)] + outs
    hbm = pl.BlockSpec(memory_space=pltpu.HBM)
    return pl.pallas_call(
        functools.partial(embed_kernel, ctx, steps, int(split)),
        out_shape=outs,
        in_specs=[hbm] * 2,
        out_specs=[hbm] * len(outs),
        scratch_shapes=[
            pltpu.VMEM((steps, slides, sub, part), BF16),
            pltpu.VMEM((steps, part, features), BF16),
            pltpu.VMEM((slides,) + shape, BF16),
            pltpu.SemaphoreType.DMA((2, steps)),
            pltpu.SemaphoreType.DMA((2, slides)),
        ],
        compiler_params=pltpu.CompilerParams(vmem_limit_bytes=60 * MIB),
        name="embed",
    )(tile_embed, w_in)


def fetch_kernel(source, after, kept, ready):
    copy = pltpu.make_async_copy(source, kept, ready)
    copy.start()
    copy.wait()


def fetch(value, after):
    hbm = pl.BlockSpec(memory_space=pltpu.HBM)
    return pl.pallas_call(
        fetch_kernel,
        out_shape=jax.ShapeDtypeStruct(value.shape, value.dtype),
        in_specs=[hbm] * 2,
        out_specs=pl.BlockSpec(memory_space=pltpu.VMEM),
        scratch_shapes=[pltpu.SemaphoreType.DMA],
        compiler_params=pltpu.CompilerParams(vmem_limit_bytes=50 * MIB),
        cost_estimate=pl.CostEstimate(flops=0, bytes_accessed=8 * 10**6, transcendentals=0),
        name="fetch",
    )(value, after)


def project(rows, weight_ref, is_valid, keys, values):
    features = weight_ref.shape[0]
    made = dot(rows, weight_ref[:, features : 2 * features])
    keys[...] = jnp.where(is_valid, made, made[0:1]).astype(BF16)
    made = dot(rows, weight_ref[:, 2 * features :])
    values[...] = jnp.where(is_valid, made, 0.0).astype(BF16)


def queries_of(rows, weight_ref):
    features = weight_ref.shape[0]
    scale = math.log2(math.e) / math.sqrt(features // HEAD_TOTAL)
    return (dot(rows, weight_ref[:, :features]) * scale).astype(BF16)


def attend(queries, keys, values, counted, put, put_total):
    count, features = queries.shape
    width = features // HEAD_TOTAL
    pair = 2 * width
    even = iota((1, pair), 1) < width
    lane = iota((1, 128), 1)
    logs = jnp.zeros((count, 128), F32)
    for at in range(0, features, pair):
        columns = slice(at, at + pair)
        both = queries[:, columns]
        key_pair = keys[:, columns]
        value_pair = jnp.concatenate([values[:, columns], counted], axis=1)
        outs = []
        for side in range(2):
            mine = even if side == 0 else ~even
            scores = lax.dot_general(jnp.where(mine, both, 0).astype(BF16), key_pair, NT, preferred_element_type=F32)
            top = jnp.max(scores, axis=-1, keepdims=True)
            weights = jnp.exp2(scores - top).astype(BF16)
            summed = dot(weights, value_pair)
            outs.append(summed)
            logs = jnp.where(lane == at // width + side, top + jnp.log2(summed[:, pair : pair + 128]), logs)
        total = jnp.where(even, outs[0][:, pair:], outs[1][:, pair:])
        out = jnp.where(even, outs[0][:, :pair], outs[1][:, :pair])
        put(columns, (out / jnp.where(total > 0, total, 1.0)).astype(BF16))
    put_total(logs)


def local_kernel(dp, ctx, block, counts_ref, *refs):
    pieces, (weight_ref, out_ref, log_ref, rows, keys, values) = refs[:dp], refs[dp:]
    me = lax.axis_index("dp")
    sub = pieces[0].shape[0]
    for other, piece in enumerate(pieces):
        rows[pl.ds(pl.multiple_of((me ^ other) * sub, sub), sub), :] = piece[...]
    count = rows.shape[0]
    each = sub // ctx
    spot = iota((count, 1), 0)
    inner = spot % sub
    position = lax.axis_index("ctx") * count + spot // sub * sub + inner % each * ctx + inner // each
    is_valid = position < counts_ref[me]
    project(rows[...], weight_ref, is_valid, keys, values)
    counted = jnp.broadcast_to(is_valid.astype(F32), (count, 128)).astype(BF16)
    for start in range(0, count, block):

        def put(columns, out):
            out_ref[start : start + block, columns] = out

        def put_total(logs):
            log_ref[start : start + block, :] = logs

        attend(queries_of(rows[start : start + block, :], weight_ref), keys, values, counted, put, put_total)


def local_attention(tile_counts, pieces, w_qkv, ctx):
    dp = len(pieces)
    sub, features = pieces[0].shape
    count = dp * sub
    vmem = pl.BlockSpec(memory_space=pltpu.VMEM)
    return pl.pallas_call(
        functools.partial(local_kernel, dp, ctx, min(256, count)),
        out_shape=[jax.ShapeDtypeStruct((count, features), BF16), jax.ShapeDtypeStruct((count, 128), F32)],
        in_specs=[pl.BlockSpec(memory_space=pltpu.SMEM)] + [vmem] * (dp + 1),
        out_specs=[vmem] * 2,
        scratch_shapes=[pltpu.VMEM((count, features), BF16)] * 3,
        compiler_params=pltpu.CompilerParams(vmem_limit_bytes=24 * MIB),
        cost_estimate=pl.CostEstimate(flops=8 * 10**9, bytes_accessed=10**7, transcendentals=0),
        name="local",
    )(tile_counts, *pieces, w_qkv)


def packed_rows(portion, features):
    return portion * (features // 128) + 16


def dilated_kernel(dp, ctx, block, sends, counts_ref, rows, weight_ref, *refs):
    out_refs, (keys, values) = refs[:-2], refs[-2:]
    me, mine = lax.axis_index("dp"), lax.axis_index("ctx")
    count, features = rows.shape
    portion = count // ctx
    each = portion // dp
    spot = iota((count, 1), 0)
    inner = spot % portion
    position = spot // portion * count + inner // each * (count // dp) + inner % each * ctx + mine
    is_valid = position < counts_ref[me]
    counted = jnp.broadcast_to(is_valid.astype(F32), (count, 128)).astype(BF16)
    project(rows[...], weight_ref, is_valid, keys, values)
    portions = block // portion
    for start in range(0, len(sends), portions):
        some = sends[start : start + portions]
        wanted = []
        for other in some:
            at = pl.multiple_of((mine ^ other) * portion, portion)
            wanted.append(rows[pl.ds(at, portion), :])

        def spread(columns, out):
            for place in range(len(some)):
                first = columns.start // 128 * portion
                out_refs[start + place][first : first + portion, :] = out[place * portion : (place + 1) * portion]

        def put_total(logs):
            high = logs.astype(BF16).astype(F32)
            low = logs - high
            lane = iota((1, 128), 1)
            both = jnp.where(lane < 16, high, pltpu.roll(low, 16, 1))
            both = jnp.where(lane < 32, both, 0.0)
            for place in range(len(some)):
                merged = both[place * portion : place * portion + 16]
                for group in range(1, portion // 16):
                    at = place * portion + group * 16
                    merged = merged + pltpu.roll(both[at : at + 16], 32 * group, 1)
                out_refs[start + place][-16:, :] = merged.astype(BF16)

        attend(queries_of(jnp.concatenate(wanted, axis=0), weight_ref), keys, values, counted, spread, put_total)


def dilated_attention(tile_counts, rows, w_qkv, dp, ctx, sends):
    count, features = rows.shape
    portion = count // ctx
    vmem = pl.BlockSpec(memory_space=pltpu.VMEM)
    return pl.pallas_call(
        functools.partial(dilated_kernel, dp, ctx, min(256, count), sends),
        out_shape=[jax.ShapeDtypeStruct((packed_rows(portion, features), 128), BF16)] * len(sends),
        in_specs=[pl.BlockSpec(memory_space=pltpu.SMEM)] + [vmem] * 2,
        out_specs=[vmem] * len(sends),
        scratch_shapes=[pltpu.VMEM((count, features), BF16)] * 2,
        compiler_params=pltpu.CompilerParams(vmem_limit_bytes=24 * MIB),
        cost_estimate=pl.CostEstimate(flops=10**6, bytes_accessed=10**4, transcendentals=0),
        name="dilated",
    )(tile_counts, rows, w_qkv)


def merge_rows(own, own_logs, features_of, logs, heads, weight):
    lane = iota((1, 128), 1)
    share = jnp.where(lane < HEAD_TOTAL, 1.0 / (1.0 + jnp.exp2(own_logs - logs)), 0.0)
    high = share.astype(BF16)
    low = (share - high.astype(F32)).astype(BF16)
    wide = dot(high, heads) + dot(low, heads)
    own = own.astype(F32)
    merged = own + wide * (features_of.astype(F32) - own)
    return dot(merged.astype(BF16), weight)


def heads_of(features):
    return (iota((128, features), 0) == iota((128, features), 1) // (features // HEAD_TOTAL)).astype(BF16)


def merge_kernel(dp, ctx, counts_ref, out_ref, log_ref, weight_ref, dilated, mixed_ref):
    me, mine = lax.axis_index("dp"), lax.axis_index("ctx")
    count, features = out_ref.shape
    sub = count // dp
    each = sub // ctx
    heads = heads_of(features)
    target, source = iota((sub, sub), 0), iota((sub, sub), 1)
    order = (target == source % each * ctx + source // each).astype(BF16)
    for part in range(dp):
        rows = slice(part * sub, (part + 1) * sub)
        logs = dilated[rows, features:].astype(F32)
        logs = logs + pltpu.roll(logs, 128 - 16, 1)
        mixed = merge_rows(out_ref[rows, :], log_ref[rows, :], dilated[rows, :features], logs, heads, weight_ref[...])
        inner = iota((sub, 1), 0)
        position = mine * count + part * sub + inner % each * ctx + inner // each
        mixed = jnp.where(position < counts_ref[me], mixed, 0.0)
        mixed_ref[0, rows, :] = dot(order, mixed.astype(BF16)).astype(BF16)


def merge(tile_counts, out, logs, w_out, received, dp, ctx):
    count, features = out.shape
    vmem = pl.BlockSpec(memory_space=pltpu.VMEM)
    return pl.pallas_call(
        functools.partial(merge_kernel, dp, ctx),
        out_shape=jax.ShapeDtypeStruct((1, count, features), BF16),
        in_specs=[pl.BlockSpec(memory_space=pltpu.SMEM)] + [vmem] * 4,
        out_specs=vmem,
        compiler_params=pltpu.CompilerParams(vmem_limit_bytes=24 * MIB),
        name="merge",
    )(tile_counts, out, logs, w_out, received)


def merge_part_kernel(dp, ctx, sends, with_others, counts_ref, out_ref, log_ref, weight_ref, *refs):
    pieces, refs = refs[: len(sends)], refs[len(sends) :]
    mixed_ref, (dilated, own, own_logs) = refs[-4], refs[-3:]
    me, mine = lax.axis_index("dp"), lax.axis_index("ctx")
    count, features = out_ref.shape
    sub = count // dp
    each = sub // ctx
    portion = count // ctx
    span = len(sends) * each
    first = (mine ^ sends[0]) // len(sends) * len(sends)
    for part in range(dp):
        at = pl.multiple_of(part * sub + first * each, each)
        own[part * span : (part + 1) * span, :] = out_ref[pl.ds(at, span), :]
        own_logs[part * span : (part + 1) * span, :] = log_ref[pl.ds(at, span), :]
    for other, piece in zip(sends, pieces):
        for part in range(dp):
            at = pl.multiple_of(part * span + ((mine ^ other) - first) * each, each)
            for block in range(features // 128):
                start = block * portion + part * each
                dilated[pl.ds(at, each), block * 128 : (block + 1) * 128] = piece[start : start + each, :]
            dilated[pl.ds(at, each), features:] = pltpu.roll(
                piece[-16:, :].astype(F32), (128 - 32 * part) % 128, 1
            ).astype(BF16)
    logs = dilated[:, features:].astype(F32)
    logs = logs + pltpu.roll(logs, 128 - 16, 1)
    mixed = merge_rows(own[...], own_logs[...], dilated[:, :features], logs, heads_of(features), weight_ref[...])
    spot = iota((dp * span, 1), 0)
    inner = spot % span
    position = mine * count + spot // span * sub + inner % each * ctx + first + inner // each
    mixed = jnp.where(position < counts_ref[me], mixed, 0.0).astype(BF16)
    target, source = iota((sub, span), 0), iota((sub, span), 1)
    order = (target == source % each * ctx + first + source // each).astype(BF16)
    for part in range(dp):
        made = dot(order, mixed[part * span : (part + 1) * span])
        rows = slice(part * sub, (part + 1) * sub)
        if with_others:
            made = made + refs[0][rows, :].astype(F32)
            mixed_ref[0, rows, :] = made.astype(BF16)
        else:
            mixed_ref[rows, :] = made.astype(BF16)


def merge_part(tile_counts, out, logs, w_out, received, dp, ctx, sends, others=()):
    count, features = out.shape
    vmem = pl.BlockSpec(memory_space=pltpu.VMEM)
    shape = (1, count, features) if others else (count, features)
    rows = count * len(sends) // ctx
    return pl.pallas_call(
        functools.partial(merge_part_kernel, dp, ctx, sends, len(others)),
        out_shape=jax.ShapeDtypeStruct(shape, BF16),
        in_specs=[pl.BlockSpec(memory_space=pltpu.SMEM)] + [vmem] * (3 + len(received) + len(others)),
        out_specs=vmem,
        scratch_shapes=[
            pltpu.VMEM((rows, features + 128), BF16),
            pltpu.VMEM((rows, features), BF16),
            pltpu.VMEM((rows, 128), F32),
        ],
        compiler_params=pltpu.CompilerParams(vmem_limit_bytes=24 * MIB),
        cost_estimate=pl.CostEstimate(flops=10**6, bytes_accessed=10**4, transcendentals=0),
        name="merge",
    )(tile_counts, out, logs, w_out, *received, *others)


def exchange(value, axis, other):
    if other == 0:
        return value
    return lax.ppermute(value, axis, [(i, i ^ other) for i in range(lax.axis_size(axis))])


def body(tile_embed, tile_counts, w_in, w_qkv, w_out):
    dp, ctx = lax.axis_size("dp"), lax.axis_size("ctx")
    slides, _, sub, _ = tile_embed.shape
    features = w_out.shape[0]
    count = sub * dp
    each = sub // ctx
    aligned = each % 16 == 0 and ctx <= 8
    made = embed(tile_embed, w_in, ctx, aligned)
    if aligned:
        by_residue, made = made[0], made[1:]
    else:
        slide_of = [lax.axis_index("dp") ^ other for other in range(dp)]
        stacked = jnp.stack(made)[jnp.stack(slide_of)]
        by_residue = stacked.reshape(slides, ctx, each, features).swapaxes(0, 1)
    pieces = [exchange(piece, "dp", other).reshape(sub, features) for other, piece in enumerate(made)]
    regrouped = lax.all_to_all(
        by_residue.reshape(ctx * dp, each, features), ("ctx", "dp"), split_axis=0, concat_axis=0, tiled=True
    ).reshape(count, features)
    w_near = fetch(w_qkv, made[0])
    portion = count // ctx
    if aligned:
        sends = (4, 5, 6, 7, 2, 3, 1, 0) if ctx == 8 else tuple(range(ctx))
        made = dilated_attention(tile_counts, regrouped, w_near, dp, ctx, sends)
        found = {other: exchange(piece, "ctx", other) for other, piece in zip(sends, made)}
        tied = lax.optimization_barrier((found[0], *pieces))
        found[0], pieces = tied[0], tied[1:]
        out, logs = local_attention(tile_counts, pieces, w_near, ctx)
        mixed = ()
        for some in ((2, 3, 1, 0), (4, 5, 6, 7)) if ctx == 8 else (sends,):
            received = [found[other] for other in some]
            mixed = (merge_part(tile_counts, out, logs, w_out, received, dp, ctx, some, mixed),)
        return mixed[0].reshape(1, count, features)
    else:
        out, logs = local_attention(tile_counts, pieces, w_near, ctx)
        made = dilated_attention(tile_counts, regrouped, w_near, dp, ctx, list(range(ctx)))
        order = jnp.stack([lax.axis_index("ctx") ^ other for other in range(ctx)])
        packed = lax.all_to_all(jnp.stack(made)[order], "ctx", split_axis=0, concat_axis=0, tiled=True)
        wide = packed[:, :-16].reshape(ctx, features // 128, portion, 128).swapaxes(1, 2).reshape(ctx, portion, features)
        lanes = packed[:, -16:].reshape(ctx, 16, 4, 32).swapaxes(1, 2)[:, : portion // 16].reshape(ctx, portion, 32)
        whole = jnp.concatenate([wide, jnp.pad(lanes, ((0, 0), (0, 0), (0, 96)))], axis=-1)
        received = whole.reshape(ctx, dp, each, -1).swapaxes(0, 1).reshape(count, -1)
        return merge(tile_counts, out, logs, w_out, received, dp, ctx)


def solution(mesh):
    in_specs = (P(None, "ctx", "dp", None), P(), P(), P(), P())
    out_specs = P("dp", "ctx", None)
    return jax.shard_map(body, mesh=mesh, in_specs=in_specs, out_specs=out_specs, check_vma=False)
```

```python
import functools
import math

import jax
import jax.numpy as jnp
from jax import lax
from jax.experimental import pallas as pl
from jax.experimental.pallas import tpu as pltpu
from jax.sharding import PartitionSpec as P

HEAD_TOTAL = 12
EPSILON = 1e-05
F32 = jnp.float32
BF16 = jnp.bfloat16
NT = (((1,), (1,)), ((), ()))
MIB = 1024 * 1024


def dot(a, b):
    return jnp.dot(a, b, preferred_element_type=F32)


def iota(shape, dim):
    return lax.broadcasted_iota(jnp.int32, shape, dim)


def embed_kernel(ctx, steps, split, x_hbm, w_hbm, *refs):
    slides, _, sub, width = x_hbm.shape
    outs = refs[: slides + split]
    x_parts, w_parts, made, arrived, sent = refs[slides + split :]
    part = width // steps
    loads = []
    for step in range(steps):
        columns = pl.ds(step * part, part)
        loads.append(
            (
                pltpu.make_async_copy(w_hbm.at[columns], w_parts.at[step], arrived.at[0, step]),
                pltpu.make_async_copy(x_hbm.at[:, 0, :, columns], x_parts.at[step], arrived.at[1, step]),
            )
        )
        for load in loads[-1]:
            load.start()
    total = None
    for step in range(steps):
        for load in loads[step]:
            load.wait()
        product = dot(x_parts[step].reshape(slides * sub, part), w_parts[step])
        total = product if total is None else total + product
    me = lax.axis_index("dp")
    each = sub // ctx
    target, source = iota((sub, sub), 0), iota((sub, sub), 1)
    order = (source == target % each * ctx + target // each).astype(BF16)
    stores = []
    for slide in range(slides):
        hidden = total[slide * sub : (slide + 1) * sub].astype(BF16).astype(F32)
        centered = hidden - jnp.mean(hidden, axis=-1, keepdims=True)
        variance = jnp.mean(centered * centered, axis=-1, keepdims=True)
        normed = (centered * lax.rsqrt(variance + EPSILON)).astype(BF16)
        made[slide] = dot(order, normed).astype(BF16).reshape(made.shape[1:])
        if split:
            stores.append(pltpu.make_async_copy(made.at[slide], outs[0].at[:, slide], sent.at[1, slide]))
            stores[-1].start()
    for other in range(slides):
        stores.append(pltpu.make_async_copy(made.at[me ^ other], outs[split + other], sent.at[0, other]))
        stores[-1].start()
    for store in stores:
        store.wait()


def embed(tile_embed, w_in, ctx, split):
    slides, _, sub, width = tile_embed.shape
    features = w_in.shape[1]
    steps = 6
    part = width // steps
    shape = (ctx, sub // ctx, features) if split else (sub, features)
    outs = [jax.ShapeDtypeStruct(shape, BF16)] * slides
    if split:
        outs = [jax.ShapeDtypeStruct((ctx, slides, sub // ctx, features), BF16)] + outs
    hbm = pl.BlockSpec(memory_space=pltpu.HBM)
    return pl.pallas_call(
        functools.partial(embed_kernel, ctx, steps, int(split)),
        out_shape=outs,
        in_specs=[hbm] * 2,
        out_specs=[hbm] * len(outs),
        scratch_shapes=[
            pltpu.VMEM((steps, slides, sub, part), BF16),
            pltpu.VMEM((steps, part, features), BF16),
            pltpu.VMEM((slides,) + shape, BF16),
            pltpu.SemaphoreType.DMA((2, steps)),
            pltpu.SemaphoreType.DMA((2, slides)),
        ],
        compiler_params=pltpu.CompilerParams(vmem_limit_bytes=60 * MIB),
        name="embed",
    )(tile_embed, w_in)


def fetch_kernel(source, after, kept, ready):
    copy = pltpu.make_async_copy(source, kept, ready)
    copy.start()
    copy.wait()


def fetch(value, after):
    hbm = pl.BlockSpec(memory_space=pltpu.HBM)
    return pl.pallas_call(
        fetch_kernel,
        out_shape=jax.ShapeDtypeStruct(value.shape, value.dtype),
        in_specs=[hbm] * 2,
        out_specs=pl.BlockSpec(memory_space=pltpu.VMEM),
        scratch_shapes=[pltpu.SemaphoreType.DMA],
        compiler_params=pltpu.CompilerParams(vmem_limit_bytes=50 * MIB),
        cost_estimate=pl.CostEstimate(flops=0, bytes_accessed=8 * 10**6, transcendentals=0),
        name="fetch",
    )(value, after)


def project(rows, weight_ref, is_valid, keys, values):
    features = weight_ref.shape[0]
    made = dot(rows, weight_ref[:, features : 2 * features])
    keys[...] = jnp.where(is_valid, made, made[0:1]).astype(BF16)
    made = dot(rows, weight_ref[:, 2 * features :])
    values[...] = jnp.where(is_valid, made, 0.0).astype(BF16)


def queries_of(rows, weight_ref):
    features = weight_ref.shape[0]
    scale = math.log2(math.e) / math.sqrt(features // HEAD_TOTAL)
    return (dot(rows, weight_ref[:, :features]) * scale).astype(BF16)


def attend(queries, keys, values, counted, put, put_total):
    count, features = queries.shape
    width = features // HEAD_TOTAL
    pair = 2 * width
    even = iota((1, pair), 1) < width
    lane = iota((1, 128), 1)
    logs = jnp.zeros((count, 128), F32)
    for at in range(0, features, pair):
        columns = slice(at, at + pair)
        both = queries[:, columns]
        key_pair = keys[:, columns]
        value_pair = jnp.concatenate([values[:, columns], counted], axis=1)
        outs = []
        for side in range(2):
            mine = even if side == 0 else ~even
            scores = lax.dot_general(jnp.where(mine, both, 0).astype(BF16), key_pair, NT, preferred_element_type=F32)
            top = jnp.max(scores, axis=-1, keepdims=True)
            weights = jnp.exp2(scores - top).astype(BF16)
            summed = dot(weights, value_pair)
            outs.append(summed)
            logs = jnp.where(lane == at // width + side, top + jnp.log2(summed[:, pair : pair + 128]), logs)
        total = jnp.where(even, outs[0][:, pair:], outs[1][:, pair:])
        out = jnp.where(even, outs[0][:, :pair], outs[1][:, :pair])
        put(columns, (out / jnp.where(total > 0, total, 1.0)).astype(BF16))
    put_total(logs)


def local_kernel(dp, ctx, block, counts_ref, *refs):
    pieces, (weight_ref, out_ref, log_ref, rows, keys, values) = refs[:dp], refs[dp:]
    me = lax.axis_index("dp")
    sub = pieces[0].shape[0]
    for other, piece in enumerate(pieces):
        rows[pl.ds(pl.multiple_of((me ^ other) * sub, sub), sub), :] = piece[...]
    count = rows.shape[0]
    each = sub // ctx
    spot = iota((count, 1), 0)
    inner = spot % sub
    position = lax.axis_index("ctx") * count + spot // sub * sub + inner % each * ctx + inner // each
    is_valid = position < counts_ref[me]
    project(rows[...], weight_ref, is_valid, keys, values)
    counted = jnp.broadcast_to(is_valid.astype(F32), (count, 128)).astype(BF16)
    for start in range(0, count, block):

        def put(columns, out):
            out_ref[start : start + block, columns] = out

        def put_total(logs):
            log_ref[start : start + block, :] = logs

        attend(queries_of(rows[start : start + block, :], weight_ref), keys, values, counted, put, put_total)


def local_attention(tile_counts, pieces, w_qkv, ctx):
    dp = len(pieces)
    sub, features = pieces[0].shape
    count = dp * sub
    vmem = pl.BlockSpec(memory_space=pltpu.VMEM)
    return pl.pallas_call(
        functools.partial(local_kernel, dp, ctx, min(256, count)),
        out_shape=[jax.ShapeDtypeStruct((count, features), BF16), jax.ShapeDtypeStruct((count, 128), F32)],
        in_specs=[pl.BlockSpec(memory_space=pltpu.SMEM)] + [vmem] * (dp + 1),
        out_specs=[vmem] * 2,
        scratch_shapes=[pltpu.VMEM((count, features), BF16)] * 3,
        compiler_params=pltpu.CompilerParams(vmem_limit_bytes=24 * MIB),
        cost_estimate=pl.CostEstimate(flops=8 * 10**9, bytes_accessed=10**7, transcendentals=0),
        name="local",
    )(tile_counts, *pieces, w_qkv)


def packed_rows(portion, features):
    return portion * (features // 128) + 16


def dilated_kernel(dp, ctx, block, sends, counts_ref, rows, weight_ref, *refs):
    out_refs, (keys, values) = refs[:-2], refs[-2:]
    out_refs = [ref.at[place] for ref, group in zip(out_refs, sends) for place in range(len(group))]
    sends = [other for group in sends for other in group]
    me, mine = lax.axis_index("dp"), lax.axis_index("ctx")
    count, features = rows.shape
    portion = count // ctx
    each = portion // dp
    spot = iota((count, 1), 0)
    inner = spot % portion
    position = spot // portion * count + inner // each * (count // dp) + inner % each * ctx + mine
    is_valid = position < counts_ref[me]
    counted = jnp.broadcast_to(is_valid.astype(F32), (count, 128)).astype(BF16)
    project(rows[...], weight_ref, is_valid, keys, values)
    portions = block // portion
    for start in range(0, len(sends), portions):
        some = sends[start : start + portions]
        wanted = []
        for other in some:
            at = pl.multiple_of((mine ^ other) * portion, portion)
            wanted.append(rows[pl.ds(at, portion), :])

        def spread(columns, out):
            for place in range(len(some)):
                first = columns.start // 128 * portion
                out_refs[start + place][first : first + portion, :] = out[place * portion : (place + 1) * portion]

        def put_total(logs):
            high = logs.astype(BF16).astype(F32)
            low = logs - high
            lane = iota((1, 128), 1)
            both = jnp.where(lane < 16, high, pltpu.roll(low, 16, 1))
            both = jnp.where(lane < 32, both, 0.0)
            for place in range(len(some)):
                merged = both[place * portion : place * portion + 16]
                for group in range(1, portion // 16):
                    at = place * portion + group * 16
                    merged = merged + pltpu.roll(both[at : at + 16], 32 * group, 1)
                out_refs[start + place][-16:, :] = merged.astype(BF16)

        attend(queries_of(jnp.concatenate(wanted, axis=0), weight_ref), keys, values, counted, spread, put_total)


def dilated_attention(tile_counts, rows, w_qkv, dp, ctx, sends):
    count, features = rows.shape
    portion = count // ctx
    vmem = pl.BlockSpec(memory_space=pltpu.VMEM)
    return pl.pallas_call(
        functools.partial(dilated_kernel, dp, ctx, min(256, count), sends),
        out_shape=[jax.ShapeDtypeStruct((len(group), packed_rows(portion, features), 128), BF16) for group in sends],
        in_specs=[pl.BlockSpec(memory_space=pltpu.SMEM)] + [vmem] * 2,
        out_specs=[vmem] * len(sends),
        scratch_shapes=[pltpu.VMEM((count, features), BF16)] * 2,
        compiler_params=pltpu.CompilerParams(vmem_limit_bytes=24 * MIB),
        cost_estimate=pl.CostEstimate(flops=10**6, bytes_accessed=10**4, transcendentals=0),
        name="dilated",
    )(tile_counts, rows, w_qkv)


def merge_rows(own, own_logs, features_of, logs, heads, weight):
    lane = iota((1, 128), 1)
    share = jnp.where(lane < HEAD_TOTAL, 1.0 / (1.0 + jnp.exp2(own_logs - logs)), 0.0)
    high = share.astype(BF16)
    low = (share - high.astype(F32)).astype(BF16)
    wide = dot(high, heads) + dot(low, heads)
    own = own.astype(F32)
    merged = own + wide * (features_of.astype(F32) - own)
    return dot(merged.astype(BF16), weight)


def heads_of(features):
    return (iota((128, features), 0) == iota((128, features), 1) // (features // HEAD_TOTAL)).astype(BF16)


def merge_kernel(dp, ctx, counts_ref, out_ref, log_ref, weight_ref, dilated, mixed_ref):
    me, mine = lax.axis_index("dp"), lax.axis_index("ctx")
    count, features = out_ref.shape
    sub = count // dp
    each = sub // ctx
    heads = heads_of(features)
    target, source = iota((sub, sub), 0), iota((sub, sub), 1)
    order = (target == source % each * ctx + source // each).astype(BF16)
    for part in range(dp):
        rows = slice(part * sub, (part + 1) * sub)
        logs = dilated[rows, features:].astype(F32)
        logs = logs + pltpu.roll(logs, 128 - 16, 1)
        mixed = merge_rows(out_ref[rows, :], log_ref[rows, :], dilated[rows, :features], logs, heads, weight_ref[...])
        inner = iota((sub, 1), 0)
        position = mine * count + part * sub + inner % each * ctx + inner // each
        mixed = jnp.where(position < counts_ref[me], mixed, 0.0)
        mixed_ref[0, rows, :] = dot(order, mixed.astype(BF16)).astype(BF16)


def merge(tile_counts, out, logs, w_out, received, dp, ctx):
    count, features = out.shape
    vmem = pl.BlockSpec(memory_space=pltpu.VMEM)
    return pl.pallas_call(
        functools.partial(merge_kernel, dp, ctx),
        out_shape=jax.ShapeDtypeStruct((1, count, features), BF16),
        in_specs=[pl.BlockSpec(memory_space=pltpu.SMEM)] + [vmem] * 4,
        out_specs=vmem,
        compiler_params=pltpu.CompilerParams(vmem_limit_bytes=24 * MIB),
        name="merge",
    )(tile_counts, out, logs, w_out, received)


def merge_part_kernel(dp, ctx, sends, with_others, counts_ref, out_ref, log_ref, weight_ref, *refs):
    pieces, refs = refs[: len(sends)], refs[len(sends) :]
    pieces = [(other, ref.at[place]) for ref, group in zip(pieces, sends) for place, other in enumerate(group)]
    sends = [other for other, _ in pieces]
    mixed_ref, (dilated, own, own_logs) = refs[-4], refs[-3:]
    me, mine = lax.axis_index("dp"), lax.axis_index("ctx")
    count, features = out_ref.shape
    sub = count // dp
    each = sub // ctx
    portion = count // ctx
    span = len(sends) * each
    first = (mine ^ sends[0]) // len(sends) * len(sends)
    for part in range(dp):
        at = pl.multiple_of(part * sub + first * each, each)
        own[part * span : (part + 1) * span, :] = out_ref[pl.ds(at, span), :]
        own_logs[part * span : (part + 1) * span, :] = log_ref[pl.ds(at, span), :]
    for other, piece in pieces:
        for part in range(dp):
            at = pl.multiple_of(part * span + ((mine ^ other) - first) * each, each)
            for block in range(features // 128):
                start = block * portion + part * each
                dilated[pl.ds(at, each), block * 128 : (block + 1) * 128] = piece[start : start + each, :]
            dilated[pl.ds(at, each), features:] = pltpu.roll(
                piece[-16:, :].astype(F32), (128 - 32 * part) % 128, 1
            ).astype(BF16)
    logs = dilated[:, features:].astype(F32)
    logs = logs + pltpu.roll(logs, 128 - 16, 1)
    mixed = merge_rows(own[...], own_logs[...], dilated[:, :features], logs, heads_of(features), weight_ref[...])
    spot = iota((dp * span, 1), 0)
    inner = spot % span
    position = mine * count + spot // span * sub + inner % each * ctx + first + inner // each
    mixed = jnp.where(position < counts_ref[me], mixed, 0.0).astype(BF16)
    target, source = iota((sub, span), 0), iota((sub, span), 1)
    order = (target == source % each * ctx + first + source // each).astype(BF16)
    for part in range(dp):
        made = dot(order, mixed[part * span : (part + 1) * span])
        rows = slice(part * sub, (part + 1) * sub)
        if with_others:
            made = made + refs[0][rows, :].astype(F32)
            mixed_ref[0, rows, :] = made.astype(BF16)
        else:
            mixed_ref[rows, :] = made.astype(BF16)


def merge_part(tile_counts, out, logs, w_out, received, dp, ctx, sends, others=()):
    count, features = out.shape
    vmem = pl.BlockSpec(memory_space=pltpu.VMEM)
    shape = (1, count, features) if others else (count, features)
    rows = count * sum(len(group) for group in sends) // ctx
    return pl.pallas_call(
        functools.partial(merge_part_kernel, dp, ctx, sends, len(others)),
        out_shape=jax.ShapeDtypeStruct(shape, BF16),
        in_specs=[pl.BlockSpec(memory_space=pltpu.SMEM)] + [vmem] * (3 + len(received) + len(others)),
        out_specs=vmem,
        scratch_shapes=[
            pltpu.VMEM((rows, features + 128), BF16),
            pltpu.VMEM((rows, features), BF16),
            pltpu.VMEM((rows, 128), F32),
        ],
        compiler_params=pltpu.CompilerParams(vmem_limit_bytes=24 * MIB),
        cost_estimate=pl.CostEstimate(flops=10**6, bytes_accessed=10**4, transcendentals=0),
        name="merge",
    )(tile_counts, out, logs, w_out, *received, *others)


def exchange(value, axis, other):
    if other == 0:
        return value
    return lax.ppermute(value, axis, [(i, i ^ other) for i in range(lax.axis_size(axis))])


def body(tile_embed, tile_counts, w_in, w_qkv, w_out):
    dp, ctx = lax.axis_size("dp"), lax.axis_size("ctx")
    slides, _, sub, _ = tile_embed.shape
    features = w_out.shape[0]
    count = sub * dp
    each = sub // ctx
    aligned = each % 16 == 0 and ctx <= 8
    made = embed(tile_embed, w_in, ctx, aligned)
    if aligned:
        by_residue, made = made[0], made[1:]
    else:
        slide_of = [lax.axis_index("dp") ^ other for other in range(dp)]
        stacked = jnp.stack(made)[jnp.stack(slide_of)]
        by_residue = stacked.reshape(slides, ctx, each, features).swapaxes(0, 1)
    pieces = [exchange(piece, "dp", other).reshape(sub, features) for other, piece in enumerate(made)]
    regrouped = lax.all_to_all(
        by_residue.reshape(ctx * dp, each, features), ("ctx", "dp"), split_axis=0, concat_axis=0, tiled=True
    ).reshape(count, features)
    regrouped, *pieces = lax.optimization_barrier((regrouped, *pieces))
    w_near = fetch(w_qkv, made[0])
    portion = count // ctx
    if aligned:
        if ctx == 8:
            far, sends = ((4,), (5,), (6,), (7,)), ((2, 3), (1,), (0,))
            *across, two_three, one, own = dilated_attention(tile_counts, regrouped, w_near, dp, ctx, far + sends)
            across = [exchange(piece, "ctx", other) for piece, (other,) in zip(across, far)]
            two_three = exchange(two_three, "ctx", 2)
            one_three = exchange(jnp.concatenate([one, two_three[1:]]), "ctx", 1)
            parts = [((2,), (0,), (1, 3)), [two_three, own, one_three]], [far, across]
        else:
            sends = tuple((other,) for other in range(ctx))
            own, *made = dilated_attention(tile_counts, regrouped, w_near, dp, ctx, sends)
            made = [exchange(piece, "ctx", other) for piece, (other,) in zip(made, sends[1:])]
            parts = ([sends, [own, *made]],)
        own, *pieces = lax.optimization_barrier((own, *pieces))
        parts[0][1][1 if ctx == 8 else 0] = own
        out, logs = local_attention(tile_counts, pieces, w_near, ctx)
        mixed = ()
        for sends, received in parts:
            mixed = (merge_part(tile_counts, out, logs, w_out, received, dp, ctx, sends, mixed),)
        return mixed[0].reshape(1, count, features)
    else:
        out, logs = local_attention(tile_counts, pieces, w_near, ctx)
        made = dilated_attention(tile_counts, regrouped, w_near, dp, ctx, (tuple(range(ctx)),))[0]
        order = jnp.stack([lax.axis_index("ctx") ^ other for other in range(ctx)])
        packed = lax.all_to_all(made[order], "ctx", split_axis=0, concat_axis=0, tiled=True)
        wide = packed[:, :-16].reshape(ctx, features // 128, portion, 128).swapaxes(1, 2).reshape(ctx, portion, features)
        lanes = packed[:, -16:].reshape(ctx, 16, 4, 32).swapaxes(1, 2)[:, : portion // 16].reshape(ctx, portion, 32)
        whole = jnp.concatenate([wide, jnp.pad(lanes, ((0, 0), (0, 0), (0, 96)))], axis=-1)
        received = whole.reshape(ctx, dp, each, -1).swapaxes(0, 1).reshape(count, -1)
        return merge(tile_counts, out, logs, w_out, received, dp, ctx)


def solution(mesh):
    in_specs = (P(None, "ctx", "dp", None), P(), P(), P(), P())
    out_specs = P("dp", "ctx", None)
    return jax.shard_map(body, mesh=mesh, in_specs=in_specs, out_specs=out_specs, check_vma=False)
```

```python
import functools
import math

import jax
import jax.numpy as jnp
from jax import lax
from jax.experimental import pallas as pl
from jax.experimental.pallas import tpu as pltpu
from jax.sharding import PartitionSpec as P

HEAD_TOTAL = 12
EPSILON = 1e-05
F32 = jnp.float32
BF16 = jnp.bfloat16
NT = (((1,), (1,)), ((), ()))
MIB = 1024 * 1024


def dot(a, b):
    return jnp.dot(a, b, preferred_element_type=F32)


def iota(shape, dim):
    return lax.broadcasted_iota(jnp.int32, shape, dim)


def embed_kernel(ctx, steps, split, x_hbm, w_hbm, *refs):
    slides, _, sub, width = x_hbm.shape
    outs = refs[: slides + split]
    early, late, weight, made, arrived, sent = refs[slides + split :]
    part = width // steps
    half = slides // 2
    loads = []
    for step in range(steps):
        columns = pl.ds(step * part, part)
        loads.append(
            (
                pltpu.make_async_copy(w_hbm.at[columns], weight.at[columns], arrived.at[0, step]),
                pltpu.make_async_copy(x_hbm.at[pl.ds(0, half), 0, :, columns], early.at[step], arrived.at[1, step]),
            )
        )
        for load in loads[-1]:
            load.start()
    last = pltpu.make_async_copy(x_hbm.at[pl.ds(half, slides - half), 0], late, arrived.at[0, steps])
    last.start()
    total = None
    for step in range(steps):
        for load in loads[step]:
            load.wait()
        product = dot(early[step].reshape(half * sub, part), weight[step * part : (step + 1) * part, :])
        total = product if total is None else total + product
    last.wait()
    totals = (total, dot(late[...].reshape((slides - half) * sub, width), weight[...]))
    me = lax.axis_index("dp")
    each = sub // ctx
    target, source = iota((sub, sub), 0), iota((sub, sub), 1)
    order = (source == target % each * ctx + target // each).astype(BF16)
    stores = []
    for slide in range(slides):
        start = slide % half * sub
        hidden = totals[slide // half][start : start + sub].astype(BF16).astype(F32)
        centered = hidden - jnp.mean(hidden, axis=-1, keepdims=True)
        variance = jnp.mean(centered * centered, axis=-1, keepdims=True)
        normed = (centered * lax.rsqrt(variance + EPSILON)).astype(BF16)
        made[slide] = dot(order, normed).astype(BF16).reshape(made.shape[1:])
        if split:
            stores.append(pltpu.make_async_copy(made.at[slide], outs[0].at[:, slide], sent.at[1, slide]))
            stores[-1].start()
    for other in range(slides):
        stores.append(pltpu.make_async_copy(made.at[me ^ other], outs[split + other], sent.at[0, other]))
        stores[-1].start()
    for store in stores:
        store.wait()


def embed(tile_embed, w_in, ctx, split):
    slides, _, sub, width = tile_embed.shape
    features = w_in.shape[1]
    steps = 6
    part = width // steps
    shape = (ctx, sub // ctx, features) if split else (sub, features)
    outs = [jax.ShapeDtypeStruct(shape, BF16)] * slides
    if split:
        outs = [jax.ShapeDtypeStruct((ctx, slides, sub // ctx, features), BF16)] + outs
    hbm = pl.BlockSpec(memory_space=pltpu.HBM)
    return pl.pallas_call(
        functools.partial(embed_kernel, ctx, steps, int(split)),
        out_shape=outs,
        in_specs=[hbm] * 2,
        out_specs=[hbm] * len(outs),
        scratch_shapes=[
            pltpu.VMEM((steps, slides // 2, sub, part), BF16),
            pltpu.VMEM((slides - slides // 2, sub, width), BF16),
            pltpu.VMEM((width, features), BF16),
            pltpu.VMEM((slides,) + shape, BF16),
            pltpu.SemaphoreType.DMA((2, steps + 1)),
            pltpu.SemaphoreType.DMA((2, slides)),
        ],
        compiler_params=pltpu.CompilerParams(vmem_limit_bytes=60 * MIB),
        name="embed",
    )(tile_embed, w_in)


def fetch_kernel(source, after, kept, ready):
    copy = pltpu.make_async_copy(source, kept, ready)
    copy.start()
    copy.wait()


def fetch(value, after):
    hbm = pl.BlockSpec(memory_space=pltpu.HBM)
    return pl.pallas_call(
        fetch_kernel,
        out_shape=jax.ShapeDtypeStruct(value.shape, value.dtype),
        in_specs=[hbm] * 2,
        out_specs=pl.BlockSpec(memory_space=pltpu.VMEM),
        scratch_shapes=[pltpu.SemaphoreType.DMA],
        compiler_params=pltpu.CompilerParams(vmem_limit_bytes=50 * MIB),
        cost_estimate=pl.CostEstimate(flops=0, bytes_accessed=8 * 10**6, transcendentals=0),
        name="fetch",
    )(value, after)


def project(rows, weight_ref, is_valid, keys, values):
    features = weight_ref.shape[0]
    made = dot(rows, weight_ref[:, features : 2 * features])
    keys[...] = jnp.where(is_valid, made, made[0:1]).astype(BF16)
    made = dot(rows, weight_ref[:, 2 * features :])
    values[...] = jnp.where(is_valid, made, 0.0).astype(BF16)


def queries_of(rows, weight_ref):
    features = weight_ref.shape[0]
    scale = math.log2(math.e) / math.sqrt(features // HEAD_TOTAL)
    return (dot(rows, weight_ref[:, :features]) * scale).astype(BF16)


def attend(queries, keys, values, counted, put, put_total):
    count, features = queries.shape
    width = features // HEAD_TOTAL
    pair = 2 * width
    even = iota((1, pair), 1) < width
    lane = iota((1, 128), 1)
    logs = jnp.zeros((count, 128), F32)
    for at in range(0, features, pair):
        columns = slice(at, at + pair)
        both = queries[:, columns]
        key_pair = keys[:, columns]
        value_pair = jnp.concatenate([values[:, columns], counted], axis=1)
        outs = []
        for side in range(2):
            mine = even if side == 0 else ~even
            scores = lax.dot_general(jnp.where(mine, both, 0).astype(BF16), key_pair, NT, preferred_element_type=F32)
            top = jnp.max(scores, axis=-1, keepdims=True)
            weights = jnp.exp2(scores - top).astype(BF16)
            summed = dot(weights, value_pair)
            outs.append(summed)
            logs = jnp.where(lane == at // width + side, top + jnp.log2(summed[:, pair : pair + 128]), logs)
        total = jnp.where(even, outs[0][:, pair:], outs[1][:, pair:])
        out = jnp.where(even, outs[0][:, :pair], outs[1][:, :pair])
        put(columns, (out / jnp.where(total > 0, total, 1.0)).astype(BF16))
    put_total(logs)


def local_kernel(dp, ctx, block, counts_ref, *refs):
    pieces, (weight_ref, out_ref, log_ref, rows, keys, values) = refs[:dp], refs[dp:]
    me = lax.axis_index("dp")
    sub = pieces[0].shape[0]
    for other, piece in enumerate(pieces):
        rows[pl.ds(pl.multiple_of((me ^ other) * sub, sub), sub), :] = piece[...]
    count = rows.shape[0]
    each = sub // ctx
    spot = iota((count, 1), 0)
    inner = spot % sub
    position = lax.axis_index("ctx") * count + spot // sub * sub + inner % each * ctx + inner // each
    is_valid = position < counts_ref[me]
    project(rows[...], weight_ref, is_valid, keys, values)
    counted = jnp.broadcast_to(is_valid.astype(F32), (count, 128)).astype(BF16)
    for start in range(0, count, block):

        def put(columns, out):
            out_ref[start : start + block, columns] = out

        def put_total(logs):
            log_ref[start : start + block, :] = logs

        attend(queries_of(rows[start : start + block, :], weight_ref), keys, values, counted, put, put_total)


def local_attention(tile_counts, pieces, w_qkv, ctx):
    dp = len(pieces)
    sub, features = pieces[0].shape
    count = dp * sub
    vmem = pl.BlockSpec(memory_space=pltpu.VMEM)
    return pl.pallas_call(
        functools.partial(local_kernel, dp, ctx, min(256, count)),
        out_shape=[jax.ShapeDtypeStruct((count, features), BF16), jax.ShapeDtypeStruct((count, 128), F32)],
        in_specs=[pl.BlockSpec(memory_space=pltpu.SMEM)] + [vmem] * (dp + 1),
        out_specs=[vmem] * 2,
        scratch_shapes=[pltpu.VMEM((count, features), BF16)] * 3,
        compiler_params=pltpu.CompilerParams(vmem_limit_bytes=24 * MIB),
        cost_estimate=pl.CostEstimate(flops=8 * 10**9, bytes_accessed=10**7, transcendentals=0),
        name="local",
    )(tile_counts, *pieces, w_qkv)


def packed_rows(portion, features):
    return portion * (features // 128) + 16


def dilated_kernel(dp, ctx, block, sends, counts_ref, rows, weight_ref, *refs):
    out_refs, (keys, values) = refs[:-2], refs[-2:]
    out_refs = [ref.at[place] for ref, group in zip(out_refs, sends) for place in range(len(group))]
    sends = [other for group in sends for other in group]
    me, mine = lax.axis_index("dp"), lax.axis_index("ctx")
    count, features = rows.shape
    portion = count // ctx
    each = portion // dp
    spot = iota((count, 1), 0)
    inner = spot % portion
    position = spot // portion * count + inner // each * (count // dp) + inner % each * ctx + mine
    is_valid = position < counts_ref[me]
    counted = jnp.broadcast_to(is_valid.astype(F32), (count, 128)).astype(BF16)
    project(rows[...], weight_ref, is_valid, keys, values)
    portions = block // portion
    for start in range(0, len(sends), portions):
        some = sends[start : start + portions]
        wanted = []
        for other in some:
            at = pl.multiple_of((mine ^ other) * portion, portion)
            wanted.append(rows[pl.ds(at, portion), :])

        def spread(columns, out):
            for place in range(len(some)):
                first = columns.start // 128 * portion
                out_refs[start + place][first : first + portion, :] = out[place * portion : (place + 1) * portion]

        def put_total(logs):
            high = logs.astype(BF16).astype(F32)
            low = logs - high
            lane = iota((1, 128), 1)
            both = jnp.where(lane < 16, high, pltpu.roll(low, 16, 1))
            both = jnp.where(lane < 32, both, 0.0)
            for place in range(len(some)):
                merged = both[place * portion : place * portion + 16]
                for group in range(1, portion // 16):
                    at = place * portion + group * 16
                    merged = merged + pltpu.roll(both[at : at + 16], 32 * group, 1)
                out_refs[start + place][-16:, :] = merged.astype(BF16)

        attend(queries_of(jnp.concatenate(wanted, axis=0), weight_ref), keys, values, counted, spread, put_total)


def dilated_attention(tile_counts, rows, w_qkv, dp, ctx, sends):
    count, features = rows.shape
    portion = count // ctx
    vmem = pl.BlockSpec(memory_space=pltpu.VMEM)
    return pl.pallas_call(
        functools.partial(dilated_kernel, dp, ctx, min(256, count), sends),
        out_shape=[jax.ShapeDtypeStruct((len(group), packed_rows(portion, features), 128), BF16) for group in sends],
        in_specs=[pl.BlockSpec(memory_space=pltpu.SMEM)] + [vmem] * 2,
        out_specs=[vmem] * len(sends),
        scratch_shapes=[pltpu.VMEM((count, features), BF16)] * 2,
        compiler_params=pltpu.CompilerParams(vmem_limit_bytes=24 * MIB),
        cost_estimate=pl.CostEstimate(flops=10**6, bytes_accessed=10**4, transcendentals=0),
        name="dilated",
    )(tile_counts, rows, w_qkv)


def merge_rows(own, own_logs, features_of, logs, heads, weight):
    lane = iota((1, 128), 1)
    share = jnp.where(lane < HEAD_TOTAL, 1.0 / (1.0 + jnp.exp2(own_logs - logs)), 0.0)
    high = share.astype(BF16)
    low = (share - high.astype(F32)).astype(BF16)
    wide = dot(high, heads) + dot(low, heads)
    own = own.astype(F32)
    merged = own + wide * (features_of.astype(F32) - own)
    return dot(merged.astype(BF16), weight)


def heads_of(features):
    return (iota((128, features), 0) == iota((128, features), 1) // (features // HEAD_TOTAL)).astype(BF16)


def merge_kernel(dp, ctx, counts_ref, out_ref, log_ref, weight_ref, dilated, mixed_ref):
    me, mine = lax.axis_index("dp"), lax.axis_index("ctx")
    count, features = out_ref.shape
    sub = count // dp
    each = sub // ctx
    heads = heads_of(features)
    target, source = iota((sub, sub), 0), iota((sub, sub), 1)
    order = (target == source % each * ctx + source // each).astype(BF16)
    for part in range(dp):
        rows = slice(part * sub, (part + 1) * sub)
        logs = dilated[rows, features:].astype(F32)
        logs = logs + pltpu.roll(logs, 128 - 16, 1)
        mixed = merge_rows(out_ref[rows, :], log_ref[rows, :], dilated[rows, :features], logs, heads, weight_ref[...])
        inner = iota((sub, 1), 0)
        position = mine * count + part * sub + inner % each * ctx + inner // each
        mixed = jnp.where(position < counts_ref[me], mixed, 0.0)
        mixed_ref[0, rows, :] = dot(order, mixed.astype(BF16)).astype(BF16)


def merge(tile_counts, out, logs, w_out, received, dp, ctx):
    count, features = out.shape
    vmem = pl.BlockSpec(memory_space=pltpu.VMEM)
    return pl.pallas_call(
        functools.partial(merge_kernel, dp, ctx),
        out_shape=jax.ShapeDtypeStruct((1, count, features), BF16),
        in_specs=[pl.BlockSpec(memory_space=pltpu.SMEM)] + [vmem] * 4,
        out_specs=vmem,
        compiler_params=pltpu.CompilerParams(vmem_limit_bytes=24 * MIB),
        name="merge",
    )(tile_counts, out, logs, w_out, received)


def merge_part_kernel(dp, ctx, sends, with_others, counts_ref, out_ref, log_ref, weight_ref, *refs):
    pieces, refs = refs[: len(sends)], refs[len(sends) :]
    pieces = [(other, ref.at[place]) for ref, group in zip(pieces, sends) for place, other in enumerate(group)]
    sends = [other for other, _ in pieces]
    mixed_ref, (dilated, own, own_logs, ready, sent) = refs[-6], refs[-5:]
    me, mine = lax.axis_index("dp"), lax.axis_index("ctx")
    count, features = out_ref.shape
    sub = count // dp
    each = sub // ctx
    portion = count // ctx
    span = len(sends) * each
    first = (mine ^ sends[0]) // len(sends) * len(sends)
    for part in range(dp):
        at = pl.multiple_of(part * sub + first * each, each)
        own[part * span : (part + 1) * span, :] = out_ref[pl.ds(at, span), :]
        own_logs[part * span : (part + 1) * span, :] = log_ref[pl.ds(at, span), :]
    for other, piece in pieces:
        for part in range(dp):
            at = pl.multiple_of(part * span + ((mine ^ other) - first) * each, each)
            for block in range(features // 128):
                start = block * portion + part * each
                dilated[pl.ds(at, each), block * 128 : (block + 1) * 128] = piece[start : start + each, :]
            dilated[pl.ds(at, each), features:] = pltpu.roll(
                piece[-16:, :].astype(F32), (128 - 32 * part) % 128, 1
            ).astype(BF16)
    logs = dilated[:, features:].astype(F32)
    logs = logs + pltpu.roll(logs, 128 - 16, 1)
    mixed = merge_rows(own[...], own_logs[...], dilated[:, :features], logs, heads_of(features), weight_ref[...])
    spot = iota((dp * span, 1), 0)
    inner = spot % span
    position = mine * count + spot // span * sub + inner % each * ctx + first + inner // each
    mixed = jnp.where(position < counts_ref[me], mixed, 0.0).astype(BF16)
    target, source = iota((sub, span), 0), iota((sub, span), 1)
    order = (target == source % each * ctx + first + source // each).astype(BF16)
    stores = []
    for part in range(dp):
        made = dot(order, mixed[part * span : (part + 1) * span])
        rows = slice(part * sub, (part + 1) * sub)
        if with_others:
            ready[rows, :] = (made + refs[0][rows, :].astype(F32)).astype(BF16)
            stores.append(pltpu.make_async_copy(ready.at[rows], mixed_ref.at[0, rows], sent.at[part]))
            stores[-1].start()
        else:
            mixed_ref[rows, :] = made.astype(BF16)
    for store in stores:
        store.wait()


def merge_part(tile_counts, out, logs, w_out, received, dp, ctx, sends, others=()):
    count, features = out.shape
    vmem = pl.BlockSpec(memory_space=pltpu.VMEM)
    shape = (1, count, features) if others else (count, features)
    rows = count * sum(len(group) for group in sends) // ctx
    return pl.pallas_call(
        functools.partial(merge_part_kernel, dp, ctx, sends, len(others)),
        out_shape=jax.ShapeDtypeStruct(shape, BF16),
        in_specs=[pl.BlockSpec(memory_space=pltpu.SMEM)] + [vmem] * (3 + len(received) + len(others)),
        out_specs=pl.BlockSpec(memory_space=pltpu.HBM) if others else vmem,
        scratch_shapes=[
            pltpu.VMEM((rows, features + 128), BF16),
            pltpu.VMEM((rows, features), BF16),
            pltpu.VMEM((rows, 128), F32),
            pltpu.VMEM((count if others else 16, features), BF16),
            pltpu.SemaphoreType.DMA((dp,)),
        ],
        compiler_params=pltpu.CompilerParams(vmem_limit_bytes=24 * MIB),
        cost_estimate=pl.CostEstimate(flops=10**6, bytes_accessed=10**4, transcendentals=0),
        name="merge",
    )(tile_counts, out, logs, w_out, *received, *others)


def exchange(value, axis, other):
    if other == 0:
        return value
    return lax.ppermute(value, axis, [(i, i ^ other) for i in range(lax.axis_size(axis))])


def body(tile_embed, tile_counts, w_in, w_qkv, w_out):
    dp, ctx = lax.axis_size("dp"), lax.axis_size("ctx")
    slides, _, sub, _ = tile_embed.shape
    features = w_out.shape[0]
    count = sub * dp
    each = sub // ctx
    aligned = each % 16 == 0 and ctx <= 8
    made = embed(tile_embed, w_in, ctx, aligned)
    if aligned:
        by_residue, made = made[0], made[1:]
    else:
        slide_of = [lax.axis_index("dp") ^ other for other in range(dp)]
        stacked = jnp.stack(made)[jnp.stack(slide_of)]
        by_residue = stacked.reshape(slides, ctx, each, features).swapaxes(0, 1)
    pieces = [exchange(piece, "dp", other).reshape(sub, features) for other, piece in enumerate(made)]
    regrouped = lax.all_to_all(
        by_residue.reshape(ctx * dp, each, features), ("ctx", "dp"), split_axis=0, concat_axis=0, tiled=True
    ).reshape(count, features)
    regrouped, *pieces = lax.optimization_barrier((regrouped, *pieces))
    w_near = fetch(w_qkv, made[0])
    portion = count // ctx
    if aligned:
        if ctx == 8:
            far, sends = ((4,), (5,), (6,), (7,)), ((2, 3), (1,), (0,))
            *across, two_three, one, own = dilated_attention(tile_counts, regrouped, w_near, dp, ctx, far + sends)
            across = [exchange(piece, "ctx", other) for piece, (other,) in zip(across, far)]
            two_three = exchange(two_three, "ctx", 2)
            one_three = exchange(jnp.concatenate([one, two_three[1:]]), "ctx", 1)
            parts = [((2,), (0,), (1, 3)), [two_three, own, one_three]], [far, across]
        else:
            sends = tuple((other,) for other in range(ctx))
            own, *made = dilated_attention(tile_counts, regrouped, w_near, dp, ctx, sends)
            made = [exchange(piece, "ctx", other) for piece, (other,) in zip(made, sends[1:])]
            parts = ([sends, [own, *made]],)
        own, *pieces = lax.optimization_barrier((own, *pieces))
        parts[0][1][1 if ctx == 8 else 0] = own
        out, logs = local_attention(tile_counts, pieces, w_near, ctx)
        mixed = ()
        for sends, received in parts:
            mixed = (merge_part(tile_counts, out, logs, w_out, received, dp, ctx, sends, mixed),)
        return mixed[0].reshape(1, count, features)
    else:
        out, logs = local_attention(tile_counts, pieces, w_near, ctx)
        made = dilated_attention(tile_counts, regrouped, w_near, dp, ctx, (tuple(range(ctx)),))[0]
        order = jnp.stack([lax.axis_index("ctx") ^ other for other in range(ctx)])
        packed = lax.all_to_all(made[order], "ctx", split_axis=0, concat_axis=0, tiled=True)
        wide = packed[:, :-16].reshape(ctx, features // 128, portion, 128).swapaxes(1, 2).reshape(ctx, portion, features)
        lanes = packed[:, -16:].reshape(ctx, 16, 4, 32).swapaxes(1, 2)[:, : portion // 16].reshape(ctx, portion, 32)
        whole = jnp.concatenate([wide, jnp.pad(lanes, ((0, 0), (0, 0), (0, 96)))], axis=-1)
        received = whole.reshape(ctx, dp, each, -1).swapaxes(0, 1).reshape(count, -1)
        return merge(tile_counts, out, logs, w_out, received, dp, ctx)


def solution(mesh):
    in_specs = (P(None, "ctx", "dp", None), P(), P(), P(), P())
    out_specs = P("dp", "ctx", None)
    return jax.shard_map(body, mesh=mesh, in_specs=in_specs, out_specs=out_specs, check_vma=False)
```

```python
import functools
import math

import jax
import jax.numpy as jnp
from jax import lax
from jax.experimental import pallas as pl
from jax.experimental.pallas import tpu as pltpu
from jax.sharding import PartitionSpec as P

HEAD_TOTAL = 12
EPSILON = 1e-05
F32 = jnp.float32
BF16 = jnp.bfloat16
NT = (((1,), (1,)), ((), ()))
MIB = 1024 * 1024


def dot(a, b):
    return jnp.dot(a, b, preferred_element_type=F32)


def iota(shape, dim):
    return lax.broadcasted_iota(jnp.int32, shape, dim)


def embed_kernel(ctx, steps, split, x_hbm, w_hbm, *refs):
    slides, _, sub, width = x_hbm.shape
    outs, (early, late, weight, made, arrived, sent) = refs[:-6], refs[-6:]
    part = width // steps
    half = slides // 2
    loads = []
    for step in range(steps):
        columns = pl.ds(step * part, part)
        loads.append(
            (
                pltpu.make_async_copy(w_hbm.at[columns], weight.at[columns], arrived.at[0, step]),
                pltpu.make_async_copy(x_hbm.at[pl.ds(0, half), 0, :, columns], early.at[step], arrived.at[1, step]),
            )
        )
        for load in loads[-1]:
            load.start()
    last = pltpu.make_async_copy(x_hbm.at[pl.ds(half, slides - half), 0], late, arrived.at[0, steps])
    last.start()
    total = None
    for step in range(steps):
        for load in loads[step]:
            load.wait()
        product = dot(early[step].reshape(half * sub, part), weight[step * part : (step + 1) * part, :])
        total = product if total is None else total + product
    last.wait()
    totals = (total, dot(late[...].reshape((slides - half) * sub, width), weight[...]))
    me = lax.axis_index("dp")
    each = sub // ctx
    target, source = iota((sub, sub), 0), iota((sub, sub), 1)
    order = (source == target % each * ctx + target // each).astype(BF16)
    stores = []
    for slide in range(slides):
        start = slide % half * sub
        hidden = totals[slide // half][start : start + sub].astype(BF16).astype(F32)
        centered = hidden - jnp.mean(hidden, axis=-1, keepdims=True)
        variance = jnp.mean(centered * centered, axis=-1, keepdims=True)
        normed = (centered * lax.rsqrt(variance + EPSILON)).astype(BF16)
        made[slide] = dot(order, normed).astype(BF16).reshape(made.shape[1:])
        if split:
            stores.append(pltpu.make_async_copy(made.at[slide], outs[0].at[:, slide], sent.at[1, slide]))
            stores[-1].start()
    if not split:
        for other in range(slides):
            stores.append(pltpu.make_async_copy(made.at[me ^ other], outs[other], sent.at[0, other]))
            stores[-1].start()
    for store in stores:
        store.wait()


def part_kernel(by_residue, *outs):
    me = lax.axis_index("dp")
    for other, out in enumerate(outs):
        out[...] = by_residue[:, me ^ other]


def part_slides(by_residue):
    ctx, slides, each, features = by_residue.shape
    vmem = pl.BlockSpec(memory_space=pltpu.VMEM)
    return pl.pallas_call(
        part_kernel,
        out_shape=[jax.ShapeDtypeStruct((ctx, each, features), BF16)] * slides,
        in_specs=[vmem],
        out_specs=[vmem] * slides,
        compiler_params=pltpu.CompilerParams(vmem_limit_bytes=16 * MIB),
        cost_estimate=pl.CostEstimate(flops=10**6, bytes_accessed=10**4, transcendentals=0),
        name="part",
    )(by_residue)


def embed(tile_embed, w_in, ctx, split):
    slides, _, sub, width = tile_embed.shape
    features = w_in.shape[1]
    steps = 6
    part = width // steps
    shape = (ctx, sub // ctx, features) if split else (sub, features)
    if split:
        outs = [jax.ShapeDtypeStruct((ctx, slides, sub // ctx, features), BF16)]
    else:
        outs = [jax.ShapeDtypeStruct(shape, BF16)] * slides
    hbm = pl.BlockSpec(memory_space=pltpu.HBM)
    return pl.pallas_call(
        functools.partial(embed_kernel, ctx, steps, int(split)),
        out_shape=outs,
        in_specs=[hbm] * 2,
        out_specs=[hbm] * len(outs),
        scratch_shapes=[
            pltpu.VMEM((steps, slides // 2, sub, part), BF16),
            pltpu.VMEM((slides - slides // 2, sub, width), BF16),
            pltpu.VMEM((width, features), BF16),
            pltpu.VMEM((slides,) + shape, BF16),
            pltpu.SemaphoreType.DMA((2, steps + 1)),
            pltpu.SemaphoreType.DMA((2, slides)),
        ],
        compiler_params=pltpu.CompilerParams(vmem_limit_bytes=60 * MIB),
        name="embed",
    )(tile_embed, w_in)


def fetch_kernel(source, after, kept, ready):
    copy = pltpu.make_async_copy(source, kept, ready)
    copy.start()
    copy.wait()


def fetch(value, after):
    hbm = pl.BlockSpec(memory_space=pltpu.HBM)
    return pl.pallas_call(
        fetch_kernel,
        out_shape=jax.ShapeDtypeStruct(value.shape, value.dtype),
        in_specs=[hbm] * 2,
        out_specs=pl.BlockSpec(memory_space=pltpu.VMEM),
        scratch_shapes=[pltpu.SemaphoreType.DMA],
        compiler_params=pltpu.CompilerParams(vmem_limit_bytes=50 * MIB),
        cost_estimate=pl.CostEstimate(flops=0, bytes_accessed=8 * 10**6, transcendentals=0),
        name="fetch",
    )(value, after)


def project(rows, weight_ref, is_valid, keys, values):
    features = weight_ref.shape[0]
    made = dot(rows, weight_ref[:, features : 2 * features])
    keys[...] = jnp.where(is_valid, made, made[0:1]).astype(BF16)
    made = dot(rows, weight_ref[:, 2 * features :])
    values[...] = jnp.where(is_valid, made, 0.0).astype(BF16)


def queries_of(rows, weight_ref):
    features = weight_ref.shape[0]
    scale = math.log2(math.e) / math.sqrt(features // HEAD_TOTAL)
    return (dot(rows, weight_ref[:, :features]) * scale).astype(BF16)


def attend(queries, keys, values, counted, put, put_total):
    count, features = queries.shape
    width = features // HEAD_TOTAL
    pair = 2 * width
    even = iota((1, pair), 1) < width
    lane = iota((1, 128), 1)
    logs = jnp.zeros((count, 128), F32)
    for at in range(0, features, pair):
        columns = slice(at, at + pair)
        both = queries[:, columns]
        key_pair = keys[:, columns]
        value_pair = jnp.concatenate([values[:, columns], counted], axis=1)
        outs = []
        for side in range(2):
            mine = even if side == 0 else ~even
            scores = lax.dot_general(jnp.where(mine, both, 0).astype(BF16), key_pair, NT, preferred_element_type=F32)
            top = jnp.max(scores, axis=-1, keepdims=True)
            weights = jnp.exp2(scores - top).astype(BF16)
            summed = dot(weights, value_pair)
            outs.append(summed)
            logs = jnp.where(lane == at // width + side, top + jnp.log2(summed[:, pair : pair + 128]), logs)
        total = jnp.where(even, outs[0][:, pair:], outs[1][:, pair:])
        out = jnp.where(even, outs[0][:, :pair], outs[1][:, :pair])
        put(columns, (out / jnp.where(total > 0, total, 1.0)).astype(BF16))
    put_total(logs)


def local_kernel(dp, ctx, block, counts_ref, *refs):
    pieces, (weight_ref, out_ref, log_ref, rows, keys, values) = refs[:dp], refs[dp:]
    me = lax.axis_index("dp")
    sub = pieces[0].shape[0]
    for other, piece in enumerate(pieces):
        rows[pl.ds(pl.multiple_of((me ^ other) * sub, sub), sub), :] = piece[...]
    count = rows.shape[0]
    each = sub // ctx
    spot = iota((count, 1), 0)
    inner = spot % sub
    position = lax.axis_index("ctx") * count + spot // sub * sub + inner % each * ctx + inner // each
    is_valid = position < counts_ref[me]
    project(rows[...], weight_ref, is_valid, keys, values)
    counted = jnp.broadcast_to(is_valid.astype(F32), (count, 128)).astype(BF16)
    for start in range(0, count, block):

        def put(columns, out):
            out_ref[start : start + block, columns] = out

        def put_total(logs):
            log_ref[start : start + block, :] = logs

        attend(queries_of(rows[start : start + block, :], weight_ref), keys, values, counted, put, put_total)


def local_attention(tile_counts, pieces, w_qkv, ctx):
    dp = len(pieces)
    sub, features = pieces[0].shape
    count = dp * sub
    vmem = pl.BlockSpec(memory_space=pltpu.VMEM)
    return pl.pallas_call(
        functools.partial(local_kernel, dp, ctx, min(256, count)),
        out_shape=[jax.ShapeDtypeStruct((count, features), BF16), jax.ShapeDtypeStruct((count, 128), F32)],
        in_specs=[pl.BlockSpec(memory_space=pltpu.SMEM)] + [vmem] * (dp + 1),
        out_specs=[vmem] * 2,
        scratch_shapes=[pltpu.VMEM((count, features), BF16)] * 3,
        compiler_params=pltpu.CompilerParams(vmem_limit_bytes=24 * MIB),
        cost_estimate=pl.CostEstimate(flops=8 * 10**9, bytes_accessed=10**7, transcendentals=0),
        name="local",
    )(tile_counts, *pieces, w_qkv)


def packed_rows(portion, features):
    return portion * (features // 128) + 16


def dilated_kernel(dp, ctx, block, sends, counts_ref, rows, weight_ref, *refs):
    out_refs, (keys, values) = refs[:-2], refs[-2:]
    out_refs = [ref.at[place] for ref, group in zip(out_refs, sends) for place in range(len(group))]
    sends = [other for group in sends for other in group]
    me, mine = lax.axis_index("dp"), lax.axis_index("ctx")
    count, features = rows.shape
    portion = count // ctx
    each = portion // dp
    spot = iota((count, 1), 0)
    inner = spot % portion
    position = spot // portion * count + inner // each * (count // dp) + inner % each * ctx + mine
    is_valid = position < counts_ref[me]
    counted = jnp.broadcast_to(is_valid.astype(F32), (count, 128)).astype(BF16)
    project(rows[...], weight_ref, is_valid, keys, values)
    portions = block // portion
    for start in range(0, len(sends), portions):
        some = sends[start : start + portions]
        wanted = []
        for other in some:
            at = pl.multiple_of((mine ^ other) * portion, portion)
            wanted.append(rows[pl.ds(at, portion), :])

        def spread(columns, out):
            for place in range(len(some)):
                first = columns.start // 128 * portion
                out_refs[start + place][first : first + portion, :] = out[place * portion : (place + 1) * portion]

        def put_total(logs):
            high = logs.astype(BF16).astype(F32)
            low = logs - high
            lane = iota((1, 128), 1)
            both = jnp.where(lane < 16, high, pltpu.roll(low, 16, 1))
            both = jnp.where(lane < 32, both, 0.0)
            for place in range(len(some)):
                merged = both[place * portion : place * portion + 16]
                for group in range(1, portion // 16):
                    at = place * portion + group * 16
                    merged = merged + pltpu.roll(both[at : at + 16], 32 * group, 1)
                out_refs[start + place][-16:, :] = merged.astype(BF16)

        attend(queries_of(jnp.concatenate(wanted, axis=0), weight_ref), keys, values, counted, spread, put_total)


def dilated_attention(tile_counts, rows, w_qkv, dp, ctx, sends):
    count, features = rows.shape
    portion = count // ctx
    vmem = pl.BlockSpec(memory_space=pltpu.VMEM)
    return pl.pallas_call(
        functools.partial(dilated_kernel, dp, ctx, min(256, count), sends),
        out_shape=[jax.ShapeDtypeStruct((len(group), packed_rows(portion, features), 128), BF16) for group in sends],
        in_specs=[pl.BlockSpec(memory_space=pltpu.SMEM)] + [vmem] * 2,
        out_specs=[vmem] * len(sends),
        scratch_shapes=[pltpu.VMEM((count, features), BF16)] * 2,
        compiler_params=pltpu.CompilerParams(vmem_limit_bytes=24 * MIB),
        cost_estimate=pl.CostEstimate(flops=10**6, bytes_accessed=10**4, transcendentals=0),
        name="dilated",
    )(tile_counts, rows, w_qkv)


def merge_rows(own, own_logs, features_of, logs, heads, weight):
    lane = iota((1, 128), 1)
    share = jnp.where(lane < HEAD_TOTAL, 1.0 / (1.0 + jnp.exp2(own_logs - logs)), 0.0)
    high = share.astype(BF16)
    low = (share - high.astype(F32)).astype(BF16)
    wide = dot(high, heads) + dot(low, heads)
    own = own.astype(F32)
    merged = own + wide * (features_of.astype(F32) - own)
    return dot(merged.astype(BF16), weight)


def heads_of(features):
    return (iota((128, features), 0) == iota((128, features), 1) // (features // HEAD_TOTAL)).astype(BF16)


def merge_kernel(dp, ctx, counts_ref, out_ref, log_ref, weight_ref, dilated, mixed_ref):
    me, mine = lax.axis_index("dp"), lax.axis_index("ctx")
    count, features = out_ref.shape
    sub = count // dp
    each = sub // ctx
    heads = heads_of(features)
    target, source = iota((sub, sub), 0), iota((sub, sub), 1)
    order = (target == source % each * ctx + source // each).astype(BF16)
    for part in range(dp):
        rows = slice(part * sub, (part + 1) * sub)
        logs = dilated[rows, features:].astype(F32)
        logs = logs + pltpu.roll(logs, 128 - 16, 1)
        mixed = merge_rows(out_ref[rows, :], log_ref[rows, :], dilated[rows, :features], logs, heads, weight_ref[...])
        inner = iota((sub, 1), 0)
        position = mine * count + part * sub + inner % each * ctx + inner // each
        mixed = jnp.where(position < counts_ref[me], mixed, 0.0)
        mixed_ref[0, rows, :] = dot(order, mixed.astype(BF16)).astype(BF16)


def merge(tile_counts, out, logs, w_out, received, dp, ctx):
    count, features = out.shape
    vmem = pl.BlockSpec(memory_space=pltpu.VMEM)
    return pl.pallas_call(
        functools.partial(merge_kernel, dp, ctx),
        out_shape=jax.ShapeDtypeStruct((1, count, features), BF16),
        in_specs=[pl.BlockSpec(memory_space=pltpu.SMEM)] + [vmem] * 4,
        out_specs=vmem,
        compiler_params=pltpu.CompilerParams(vmem_limit_bytes=24 * MIB),
        name="merge",
    )(tile_counts, out, logs, w_out, received)


def merge_part_kernel(dp, ctx, sends, with_others, counts_ref, out_ref, log_ref, weight_ref, *refs):
    pieces, refs = refs[: len(sends)], refs[len(sends) :]
    pieces = [(other, ref.at[place]) for ref, group in zip(pieces, sends) for place, other in enumerate(group)]
    sends = [other for other, _ in pieces]
    mixed_ref, (dilated, own, own_logs, ready, sent) = refs[-6], refs[-5:]
    me, mine = lax.axis_index("dp"), lax.axis_index("ctx")
    count, features = out_ref.shape
    sub = count // dp
    each = sub // ctx
    portion = count // ctx
    span = len(sends) * each
    first = (mine ^ sends[0]) // len(sends) * len(sends)
    for part in range(dp):
        at = pl.multiple_of(part * sub + first * each, each)
        own[part * span : (part + 1) * span, :] = out_ref[pl.ds(at, span), :]
        own_logs[part * span : (part + 1) * span, :] = log_ref[pl.ds(at, span), :]
    for other, piece in pieces:
        for part in range(dp):
            at = pl.multiple_of(part * span + ((mine ^ other) - first) * each, each)
            for block in range(features // 128):
                start = block * portion + part * each
                dilated[pl.ds(at, each), block * 128 : (block + 1) * 128] = piece[start : start + each, :]
            dilated[pl.ds(at, each), features:] = pltpu.roll(
                piece[-16:, :].astype(F32), (128 - 32 * part) % 128, 1
            ).astype(BF16)
    logs = dilated[:, features:].astype(F32)
    logs = logs + pltpu.roll(logs, 128 - 16, 1)
    mixed = merge_rows(own[...], own_logs[...], dilated[:, :features], logs, heads_of(features), weight_ref[...])
    spot = iota((dp * span, 1), 0)
    inner = spot % span
    position = mine * count + spot // span * sub + inner % each * ctx + first + inner // each
    mixed = jnp.where(position < counts_ref[me], mixed, 0.0).astype(BF16)
    target, source = iota((sub, span), 0), iota((sub, span), 1)
    order = (target == source % each * ctx + first + source // each).astype(BF16)
    stores = []
    for part in range(dp):
        made = dot(order, mixed[part * span : (part + 1) * span])
        rows = slice(part * sub, (part + 1) * sub)
        if with_others:
            ready[rows, :] = (made + refs[0][rows, :].astype(F32)).astype(BF16)
            stores.append(pltpu.make_async_copy(ready.at[rows], mixed_ref.at[0, rows], sent.at[part]))
            stores[-1].start()
        else:
            mixed_ref[rows, :] = made.astype(BF16)
    for store in stores:
        store.wait()


def merge_part(tile_counts, out, logs, w_out, received, dp, ctx, sends, others=()):
    count, features = out.shape
    vmem = pl.BlockSpec(memory_space=pltpu.VMEM)
    shape = (1, count, features) if others else (count, features)
    rows = count * sum(len(group) for group in sends) // ctx
    return pl.pallas_call(
        functools.partial(merge_part_kernel, dp, ctx, sends, len(others)),
        out_shape=jax.ShapeDtypeStruct(shape, BF16),
        in_specs=[pl.BlockSpec(memory_space=pltpu.SMEM)] + [vmem] * (3 + len(received) + len(others)),
        out_specs=pl.BlockSpec(memory_space=pltpu.HBM) if others else vmem,
        scratch_shapes=[
            pltpu.VMEM((rows, features + 128), BF16),
            pltpu.VMEM((rows, features), BF16),
            pltpu.VMEM((rows, 128), F32),
            pltpu.VMEM((count if others else 16, features), BF16),
            pltpu.SemaphoreType.DMA((dp,)),
        ],
        compiler_params=pltpu.CompilerParams(vmem_limit_bytes=24 * MIB),
        cost_estimate=pl.CostEstimate(flops=10**6, bytes_accessed=10**4, transcendentals=0),
        name="merge",
    )(tile_counts, out, logs, w_out, *received, *others)


def exchange(value, axis, other):
    if other == 0:
        return value
    return lax.ppermute(value, axis, [(i, i ^ other) for i in range(lax.axis_size(axis))])


def body(tile_embed, tile_counts, w_in, w_qkv, w_out):
    dp, ctx = lax.axis_size("dp"), lax.axis_size("ctx")
    slides, _, sub, _ = tile_embed.shape
    features = w_out.shape[0]
    count = sub * dp
    each = sub // ctx
    aligned = each % 16 == 0 and ctx <= 8
    made = embed(tile_embed, w_in, ctx, aligned)
    if aligned:
        by_residue, made = made[0], part_slides(made[0])
    else:
        slide_of = [lax.axis_index("dp") ^ other for other in range(dp)]
        stacked = jnp.stack(made)[jnp.stack(slide_of)]
        by_residue = stacked.reshape(slides, ctx, each, features).swapaxes(0, 1)
    pieces = [exchange(piece, "dp", other).reshape(sub, features) for other, piece in enumerate(made)]
    regrouped = lax.all_to_all(
        by_residue.reshape(ctx * dp, each, features), ("ctx", "dp"), split_axis=0, concat_axis=0, tiled=True
    ).reshape(count, features)
    regrouped, *pieces = lax.optimization_barrier((regrouped, *pieces))
    w_near = fetch(w_qkv, made[0])
    portion = count // ctx
    if aligned:
        if ctx == 8:
            far, sends = ((4,), (5,), (6,), (7,)), ((2, 3), (1,), (0,))
            *across, two_three, one, own = dilated_attention(tile_counts, regrouped, w_near, dp, ctx, far + sends)
            across = [exchange(piece, "ctx", other) for piece, (other,) in zip(across, far)]
            two_three = exchange(two_three, "ctx", 2)
            one_three = exchange(jnp.concatenate([one, two_three[1:]]), "ctx", 1)
            parts = [((2,), (0,), (1, 3)), [two_three, own, one_three]], [far, across]
        else:
            sends = tuple((other,) for other in range(ctx))
            own, *made = dilated_attention(tile_counts, regrouped, w_near, dp, ctx, sends)
            made = [exchange(piece, "ctx", other) for piece, (other,) in zip(made, sends[1:])]
            parts = ([sends, [own, *made]],)
        own, *pieces = lax.optimization_barrier((own, *pieces))
        parts[0][1][1 if ctx == 8 else 0] = own
        out, logs = local_attention(tile_counts, pieces, w_near, ctx)
        mixed = ()
        for sends, received in parts:
            mixed = (merge_part(tile_counts, out, logs, w_out, received, dp, ctx, sends, mixed),)
        return mixed[0].reshape(1, count, features)
    else:
        out, logs = local_attention(tile_counts, pieces, w_near, ctx)
        made = dilated_attention(tile_counts, regrouped, w_near, dp, ctx, (tuple(range(ctx)),))[0]
        order = jnp.stack([lax.axis_index("ctx") ^ other for other in range(ctx)])
        packed = lax.all_to_all(made[order], "ctx", split_axis=0, concat_axis=0, tiled=True)
        wide = packed[:, :-16].reshape(ctx, features // 128, portion, 128).swapaxes(1, 2).reshape(ctx, portion, features)
        lanes = packed[:, -16:].reshape(ctx, 16, 4, 32).swapaxes(1, 2)[:, : portion // 16].reshape(ctx, portion, 32)
        whole = jnp.concatenate([wide, jnp.pad(lanes, ((0, 0), (0, 0), (0, 96)))], axis=-1)
        received = whole.reshape(ctx, dp, each, -1).swapaxes(0, 1).reshape(count, -1)
        return merge(tile_counts, out, logs, w_out, received, dp, ctx)


def solution(mesh):
    in_specs = (P(None, "ctx", "dp", None), P(), P(), P(), P())
    out_specs = P("dp", "ctx", None)
    return jax.shard_map(body, mesh=mesh, in_specs=in_specs, out_specs=out_specs, check_vma=False)
```

```python
import functools
import math

import jax
import jax.numpy as jnp
from jax import lax
from jax.experimental import pallas as pl
from jax.experimental.pallas import tpu as pltpu
from jax.sharding import PartitionSpec as P

HEAD_TOTAL = 12
EPSILON = 1e-05
F32 = jnp.float32
BF16 = jnp.bfloat16
NT = (((1,), (1,)), ((), ()))
MIB = 1024 * 1024


def dot(a, b):
    return jnp.dot(a, b, preferred_element_type=F32)


def iota(shape, dim):
    return lax.broadcasted_iota(jnp.int32, shape, dim)


def embed_kernel(ctx, steps, split, x_hbm, w_hbm, *refs):
    slides, _, sub, width = x_hbm.shape
    outs, (early, late, weight, made, arrived, sent) = refs[:-6], refs[-6:]
    part = width // steps
    half = slides // 2
    loads = []
    for step in range(steps):
        columns = pl.ds(step * part, part)
        loads.append(
            (
                pltpu.make_async_copy(w_hbm.at[columns], weight.at[columns], arrived.at[0, step]),
                pltpu.make_async_copy(x_hbm.at[pl.ds(0, half), 0, :, columns], early.at[step], arrived.at[1, step]),
            )
        )
        for load in loads[-1]:
            load.start()
    last = pltpu.make_async_copy(x_hbm.at[pl.ds(half, slides - half), 0], late, arrived.at[0, steps])
    last.start()
    total = None
    for step in range(steps):
        for load in loads[step]:
            load.wait()
        product = dot(early[step].reshape(half * sub, part), weight[step * part : (step + 1) * part, :])
        total = product if total is None else total + product
    last.wait()
    totals = (total, dot(late[...].reshape((slides - half) * sub, width), weight[...]))
    me = lax.axis_index("dp")
    each = sub // ctx
    target, source = iota((sub, sub), 0), iota((sub, sub), 1)
    order = (source == target % each * ctx + target // each).astype(BF16)
    stores = []
    for slide in range(slides):
        start = slide % half * sub
        hidden = totals[slide // half][start : start + sub].astype(BF16).astype(F32)
        centered = hidden - jnp.mean(hidden, axis=-1, keepdims=True)
        variance = jnp.mean(centered * centered, axis=-1, keepdims=True)
        normed = (centered * lax.rsqrt(variance + EPSILON)).astype(BF16)
        made[slide] = dot(order, normed).astype(BF16).reshape(made.shape[1:])
        if split:
            stores.append(pltpu.make_async_copy(made.at[slide], outs[0].at[:, slide], sent.at[1, slide]))
            stores[-1].start()
    if not split:
        for other in range(slides):
            stores.append(pltpu.make_async_copy(made.at[me ^ other], outs[other], sent.at[0, other]))
            stores[-1].start()
    for store in stores:
        store.wait()


def part_kernel(by_residue, *outs):
    me = lax.axis_index("dp")
    for other, out in enumerate(outs):
        out[...] = by_residue[:, me ^ other]


def part_slides(by_residue):
    ctx, slides, each, features = by_residue.shape
    vmem = pl.BlockSpec(memory_space=pltpu.VMEM)
    return pl.pallas_call(
        part_kernel,
        out_shape=[jax.ShapeDtypeStruct((ctx, each, features), BF16)] * slides,
        in_specs=[vmem],
        out_specs=[vmem] * slides,
        compiler_params=pltpu.CompilerParams(vmem_limit_bytes=16 * MIB),
        cost_estimate=pl.CostEstimate(flops=10**6, bytes_accessed=10**4, transcendentals=0),
        name="part",
    )(by_residue)


def embed(tile_embed, w_in, ctx, split):
    slides, _, sub, width = tile_embed.shape
    features = w_in.shape[1]
    steps = 6
    part = width // steps
    shape = (ctx, sub // ctx, features) if split else (sub, features)
    if split:
        outs = [jax.ShapeDtypeStruct((ctx, slides, sub // ctx, features), BF16)]
    else:
        outs = [jax.ShapeDtypeStruct(shape, BF16)] * slides
    hbm = pl.BlockSpec(memory_space=pltpu.HBM)
    return pl.pallas_call(
        functools.partial(embed_kernel, ctx, steps, int(split)),
        out_shape=outs,
        in_specs=[hbm] * 2,
        out_specs=[hbm] * len(outs),
        scratch_shapes=[
            pltpu.VMEM((steps, slides // 2, sub, part), BF16),
            pltpu.VMEM((slides - slides // 2, sub, width), BF16),
            pltpu.VMEM((width, features), BF16),
            pltpu.VMEM((slides,) + shape, BF16),
            pltpu.SemaphoreType.DMA((2, steps + 1)),
            pltpu.SemaphoreType.DMA((2, slides)),
        ],
        compiler_params=pltpu.CompilerParams(vmem_limit_bytes=60 * MIB),
        name="embed",
    )(tile_embed, w_in)


def fetch_kernel(source, after, kept, ready):
    copy = pltpu.make_async_copy(source, kept, ready)
    copy.start()
    copy.wait()


def fetch(value, after):
    hbm = pl.BlockSpec(memory_space=pltpu.HBM)
    return pl.pallas_call(
        fetch_kernel,
        out_shape=jax.ShapeDtypeStruct(value.shape, value.dtype),
        in_specs=[hbm] * 2,
        out_specs=pl.BlockSpec(memory_space=pltpu.VMEM),
        scratch_shapes=[pltpu.SemaphoreType.DMA],
        compiler_params=pltpu.CompilerParams(vmem_limit_bytes=50 * MIB),
        cost_estimate=pl.CostEstimate(flops=0, bytes_accessed=8 * 10**6, transcendentals=0),
        name="fetch",
    )(value, after)


def project(rows, weight_ref, is_valid, keys, values):
    features = weight_ref.shape[0]
    made = dot(rows, weight_ref[:, features : 2 * features])
    keys[...] = jnp.where(is_valid, made, made[0:1]).astype(BF16)
    made = dot(rows, weight_ref[:, 2 * features :])
    values[...] = jnp.where(is_valid, made, 0.0).astype(BF16)


def queries_of(rows, weight_ref):
    features = weight_ref.shape[0]
    scale = math.log2(math.e) / math.sqrt(features // HEAD_TOTAL)
    return (dot(rows, weight_ref[:, :features]) * scale).astype(BF16)


def attend(queries, keys, values, counted, put, put_total):
    count, features = queries.shape
    width = features // HEAD_TOTAL
    pair = 2 * width
    even = iota((1, pair), 1) < width
    lane = iota((1, 128), 1)
    logs = jnp.zeros((count, 128), F32)
    for at in range(0, features, pair):
        columns = slice(at, at + pair)
        both = queries[:, columns]
        key_pair = keys[:, columns]
        value_pair = jnp.concatenate([values[:, columns], counted], axis=1)
        outs = []
        for side in range(2):
            mine = even if side == 0 else ~even
            scores = lax.dot_general(jnp.where(mine, both, 0).astype(BF16), key_pair, NT, preferred_element_type=F32)
            top = jnp.max(scores, axis=-1, keepdims=True)
            weights = jnp.exp2(scores - top).astype(BF16)
            summed = dot(weights, value_pair)
            outs.append(summed)
            logs = jnp.where(lane == at // width + side, top + jnp.log2(summed[:, pair : pair + 128]), logs)
        total = jnp.where(even, outs[0][:, pair:], outs[1][:, pair:])
        out = jnp.where(even, outs[0][:, :pair], outs[1][:, :pair])
        put(columns, (out / jnp.where(total > 0, total, 1.0)).astype(BF16))
    put_total(logs)


def local_kernel(dp, ctx, block, counts_ref, *refs):
    pieces, (weight_ref, out_ref, log_ref, rows, keys, values) = refs[:dp], refs[dp:]
    me = lax.axis_index("dp")
    sub = pieces[0].shape[0]
    for other, piece in enumerate(pieces):
        rows[pl.ds(pl.multiple_of((me ^ other) * sub, sub), sub), :] = piece[...]
    count = rows.shape[0]
    each = sub // ctx
    spot = iota((count, 1), 0)
    inner = spot % sub
    position = lax.axis_index("ctx") * count + spot // sub * sub + inner % each * ctx + inner // each
    is_valid = position < counts_ref[me]
    project(rows[...], weight_ref, is_valid, keys, values)
    counted = jnp.broadcast_to(is_valid.astype(F32), (count, 128)).astype(BF16)
    for start in range(0, count, block):

        def put(columns, out):
            out_ref[start : start + block, columns] = out

        def put_total(logs):
            log_ref[start : start + block, :] = logs

        attend(queries_of(rows[start : start + block, :], weight_ref), keys, values, counted, put, put_total)


def local_attention(tile_counts, pieces, w_qkv, ctx):
    dp = len(pieces)
    sub, features = pieces[0].shape
    count = dp * sub
    vmem = pl.BlockSpec(memory_space=pltpu.VMEM)
    return pl.pallas_call(
        functools.partial(local_kernel, dp, ctx, min(256, count)),
        out_shape=[jax.ShapeDtypeStruct((count, features), BF16), jax.ShapeDtypeStruct((count, 128), F32)],
        in_specs=[pl.BlockSpec(memory_space=pltpu.SMEM)] + [vmem] * (dp + 1),
        out_specs=[vmem] * 2,
        scratch_shapes=[pltpu.VMEM((count, features), BF16)] * 3,
        compiler_params=pltpu.CompilerParams(vmem_limit_bytes=24 * MIB),
        cost_estimate=pl.CostEstimate(flops=8 * 10**9, bytes_accessed=10**7, transcendentals=0),
        name="local",
    )(tile_counts, *pieces, w_qkv)


def packed_rows(portion, features):
    return portion * (features // 128) + 16


def dilated_kernel(dp, ctx, block, sends, counts_ref, rows, weight_ref, *refs):
    out_refs, (keys, values) = refs[:-2], refs[-2:]
    out_refs = [ref.at[place] for ref, group in zip(out_refs, sends) for place in range(len(group))]
    sends = [other for group in sends for other in group]
    me, mine = lax.axis_index("dp"), lax.axis_index("ctx")
    count, features = rows.shape
    portion = count // ctx
    each = portion // dp
    spot = iota((count, 1), 0)
    inner = spot % portion
    position = spot // portion * count + inner // each * (count // dp) + inner % each * ctx + mine
    is_valid = position < counts_ref[me]
    counted = jnp.broadcast_to(is_valid.astype(F32), (count, 128)).astype(BF16)
    project(rows[...], weight_ref, is_valid, keys, values)
    portions = block // portion
    for start in range(0, len(sends), portions):
        some = sends[start : start + portions]
        wanted = []
        for other in some:
            at = pl.multiple_of((mine ^ other) * portion, portion)
            wanted.append(rows[pl.ds(at, portion), :])

        def spread(columns, out):
            for place in range(len(some)):
                first = columns.start // 128 * portion
                out_refs[start + place][first : first + portion, :] = out[place * portion : (place + 1) * portion]

        def put_total(logs):
            high = logs.astype(BF16).astype(F32)
            low = logs - high
            lane = iota((1, 128), 1)
            both = jnp.where(lane < 16, high, pltpu.roll(low, 16, 1))
            both = jnp.where(lane < 32, both, 0.0)
            for place in range(len(some)):
                merged = both[place * portion : place * portion + 16]
                for group in range(1, portion // 16):
                    at = place * portion + group * 16
                    merged = merged + pltpu.roll(both[at : at + 16], 32 * group, 1)
                out_refs[start + place][-16:, :] = merged.astype(BF16)

        attend(queries_of(jnp.concatenate(wanted, axis=0), weight_ref), keys, values, counted, spread, put_total)


def dilated_attention(tile_counts, rows, w_qkv, dp, ctx, sends):
    count, features = rows.shape
    portion = count // ctx
    vmem = pl.BlockSpec(memory_space=pltpu.VMEM)
    return pl.pallas_call(
        functools.partial(dilated_kernel, dp, ctx, min(256, count), sends),
        out_shape=[jax.ShapeDtypeStruct((len(group), packed_rows(portion, features), 128), BF16) for group in sends],
        in_specs=[pl.BlockSpec(memory_space=pltpu.SMEM)] + [vmem] * 2,
        out_specs=[vmem] * len(sends),
        scratch_shapes=[pltpu.VMEM((count, features), BF16)] * 2,
        compiler_params=pltpu.CompilerParams(vmem_limit_bytes=24 * MIB),
        cost_estimate=pl.CostEstimate(flops=10**6, bytes_accessed=10**4, transcendentals=0),
        name="dilated",
    )(tile_counts, rows, w_qkv)


def merge_rows(own, own_logs, features_of, logs, heads, weight):
    lane = iota((1, 128), 1)
    share = jnp.where(lane < HEAD_TOTAL, 1.0 / (1.0 + jnp.exp2(own_logs - logs)), 0.0)
    high = share.astype(BF16).astype(F32)
    wide = dot((high + pltpu.roll(share - high, 16, 1)).astype(BF16), heads)
    own = own.astype(F32)
    merged = own + wide * (features_of.astype(F32) - own)
    return dot(merged.astype(BF16), weight)


def heads_of(features):
    lane = iota((128, features), 0)
    return ((lane % 16 == iota((128, features), 1) // (features // HEAD_TOTAL)) & (lane < 32)).astype(BF16)


def merge_kernel(dp, ctx, counts_ref, out_ref, log_ref, weight_ref, dilated, mixed_ref):
    me, mine = lax.axis_index("dp"), lax.axis_index("ctx")
    count, features = out_ref.shape
    sub = count // dp
    each = sub // ctx
    heads = heads_of(features)
    target, source = iota((sub, sub), 0), iota((sub, sub), 1)
    order = (target == source % each * ctx + source // each).astype(BF16)
    for part in range(dp):
        rows = slice(part * sub, (part + 1) * sub)
        logs = dilated[rows, features:].astype(F32)
        logs = logs + pltpu.roll(logs, 128 - 16, 1)
        mixed = merge_rows(out_ref[rows, :], log_ref[rows, :], dilated[rows, :features], logs, heads, weight_ref[...])
        inner = iota((sub, 1), 0)
        position = mine * count + part * sub + inner % each * ctx + inner // each
        mixed = jnp.where(position < counts_ref[me], mixed, 0.0)
        mixed_ref[0, rows, :] = dot(order, mixed.astype(BF16)).astype(BF16)


def merge(tile_counts, out, logs, w_out, received, dp, ctx):
    count, features = out.shape
    vmem = pl.BlockSpec(memory_space=pltpu.VMEM)
    return pl.pallas_call(
        functools.partial(merge_kernel, dp, ctx),
        out_shape=jax.ShapeDtypeStruct((1, count, features), BF16),
        in_specs=[pl.BlockSpec(memory_space=pltpu.SMEM)] + [vmem] * 4,
        out_specs=vmem,
        compiler_params=pltpu.CompilerParams(vmem_limit_bytes=24 * MIB),
        name="merge",
    )(tile_counts, out, logs, w_out, received)


def merge_part_kernel(dp, ctx, sends, with_others, counts_ref, out_ref, log_ref, weight_ref, *refs):
    pieces, refs = refs[: len(sends)], refs[len(sends) :]
    pieces = [(other, ref.at[place]) for ref, group in zip(pieces, sends) for place, other in enumerate(group)]
    sends = [other for other, _ in pieces]
    mixed_ref, (dilated, own, own_logs, ready, sent) = refs[-6], refs[-5:]
    me, mine = lax.axis_index("dp"), lax.axis_index("ctx")
    count, features = out_ref.shape
    sub = count // dp
    each = sub // ctx
    portion = count // ctx
    span = len(sends) * each
    first = (mine ^ sends[0]) // len(sends) * len(sends)
    for part in range(dp):
        at = pl.multiple_of(part * sub + first * each, each)
        own[part * span : (part + 1) * span, :] = out_ref[pl.ds(at, span), :]
        own_logs[part * span : (part + 1) * span, :] = log_ref[pl.ds(at, span), :]
    for other, piece in pieces:
        for part in range(dp):
            at = pl.multiple_of(part * span + ((mine ^ other) - first) * each, each)
            for block in range(features // 128):
                start = block * portion + part * each
                dilated[pl.ds(at, each), block * 128 : (block + 1) * 128] = piece[start : start + each, :]
            dilated[pl.ds(at, each), features:] = pltpu.roll(
                piece[-16:, :].astype(F32), (128 - 32 * part) % 128, 1
            ).astype(BF16)
    logs = dilated[:, features:].astype(F32)
    logs = logs + pltpu.roll(logs, 128 - 16, 1)
    mixed = merge_rows(own[...], own_logs[...], dilated[:, :features], logs, heads_of(features), weight_ref[...])
    spot = iota((dp * span, 1), 0)
    inner = spot % span
    position = mine * count + spot // span * sub + inner % each * ctx + first + inner // each
    mixed = jnp.where(position < counts_ref[me], mixed, 0.0).astype(BF16)
    target, source = iota((sub, span), 0), iota((sub, span), 1)
    order = (target == source % each * ctx + first + source // each).astype(BF16)
    stores = []
    for part in range(dp):
        made = dot(order, mixed[part * span : (part + 1) * span])
        rows = slice(part * sub, (part + 1) * sub)
        if with_others:
            ready[rows, :] = (made + refs[0][rows, :].astype(F32)).astype(BF16)
            stores.append(pltpu.make_async_copy(ready.at[rows], mixed_ref.at[0, rows], sent.at[part]))
            stores[-1].start()
        else:
            mixed_ref[rows, :] = made.astype(BF16)
    for store in stores:
        store.wait()


def merge_part(tile_counts, out, logs, w_out, received, dp, ctx, sends, others=()):
    count, features = out.shape
    vmem = pl.BlockSpec(memory_space=pltpu.VMEM)
    shape = (1, count, features) if others else (count, features)
    rows = count * sum(len(group) for group in sends) // ctx
    return pl.pallas_call(
        functools.partial(merge_part_kernel, dp, ctx, sends, len(others)),
        out_shape=jax.ShapeDtypeStruct(shape, BF16),
        in_specs=[pl.BlockSpec(memory_space=pltpu.SMEM)] + [vmem] * (3 + len(received) + len(others)),
        out_specs=pl.BlockSpec(memory_space=pltpu.HBM) if others else vmem,
        scratch_shapes=[
            pltpu.VMEM((rows, features + 128), BF16),
            pltpu.VMEM((rows, features), BF16),
            pltpu.VMEM((rows, 128), F32),
            pltpu.VMEM((count if others else 16, features), BF16),
            pltpu.SemaphoreType.DMA((dp,)),
        ],
        compiler_params=pltpu.CompilerParams(vmem_limit_bytes=24 * MIB),
        cost_estimate=pl.CostEstimate(flops=10**6, bytes_accessed=10**4, transcendentals=0),
        name="merge",
    )(tile_counts, out, logs, w_out, *received, *others)


def exchange(value, axis, other):
    if other == 0:
        return value
    return lax.ppermute(value, axis, [(i, i ^ other) for i in range(lax.axis_size(axis))])


def body(tile_embed, tile_counts, w_in, w_qkv, w_out):
    dp, ctx = lax.axis_size("dp"), lax.axis_size("ctx")
    slides, _, sub, _ = tile_embed.shape
    features = w_out.shape[0]
    count = sub * dp
    each = sub // ctx
    aligned = each % 16 == 0 and ctx <= 8
    made = embed(tile_embed, w_in, ctx, aligned)
    if aligned:
        by_residue, made = made[0], part_slides(made[0])
    else:
        slide_of = [lax.axis_index("dp") ^ other for other in range(dp)]
        stacked = jnp.stack(made)[jnp.stack(slide_of)]
        by_residue = stacked.reshape(slides, ctx, each, features).swapaxes(0, 1)
    pieces = [exchange(piece, "dp", other).reshape(sub, features) for other, piece in enumerate(made)]
    regrouped = lax.all_to_all(
        by_residue.reshape(ctx * dp, each, features), ("ctx", "dp"), split_axis=0, concat_axis=0, tiled=True
    ).reshape(count, features)
    regrouped, *pieces = lax.optimization_barrier((regrouped, *pieces))
    w_near = fetch(w_qkv, made[0])
    portion = count // ctx
    if aligned:
        if ctx == 8:
            far, sends = ((4,), (5,), (6,), (7,)), ((2, 3), (1,), (0,))
            *across, two_three, one, own = dilated_attention(tile_counts, regrouped, w_near, dp, ctx, far + sends)
            across = [exchange(piece, "ctx", other) for piece, (other,) in zip(across, far)]
            two_three = exchange(two_three, "ctx", 2)
            one_three = exchange(jnp.concatenate([one, two_three[1:]]), "ctx", 1)
            parts = [((2,), (0,), (1, 3)), [two_three, own, one_three]], [far, across]
        else:
            sends = tuple((other,) for other in range(ctx))
            own, *made = dilated_attention(tile_counts, regrouped, w_near, dp, ctx, sends)
            made = [exchange(piece, "ctx", other) for piece, (other,) in zip(made, sends[1:])]
            parts = ([sends, [own, *made]],)
        own, *pieces = lax.optimization_barrier((own, *pieces))
        parts[0][1][1 if ctx == 8 else 0] = own
        out, logs = local_attention(tile_counts, pieces, w_near, ctx)
        mixed = ()
        for sends, received in parts:
            mixed = (merge_part(tile_counts, out, logs, w_out, received, dp, ctx, sends, mixed),)
        return mixed[0].reshape(1, count, features)
    else:
        out, logs = local_attention(tile_counts, pieces, w_near, ctx)
        made = dilated_attention(tile_counts, regrouped, w_near, dp, ctx, (tuple(range(ctx)),))[0]
        order = jnp.stack([lax.axis_index("ctx") ^ other for other in range(ctx)])
        packed = lax.all_to_all(made[order], "ctx", split_axis=0, concat_axis=0, tiled=True)
        wide = packed[:, :-16].reshape(ctx, features // 128, portion, 128).swapaxes(1, 2).reshape(ctx, portion, features)
        lanes = packed[:, -16:].reshape(ctx, 16, 4, 32).swapaxes(1, 2)[:, : portion // 16].reshape(ctx, portion, 32)
        whole = jnp.concatenate([wide, jnp.pad(lanes, ((0, 0), (0, 0), (0, 96)))], axis=-1)
        received = whole.reshape(ctx, dp, each, -1).swapaxes(0, 1).reshape(count, -1)
        return merge(tile_counts, out, logs, w_out, received, dp, ctx)


def solution(mesh):
    in_specs = (P(None, "ctx", "dp", None), P(), P(), P(), P())
    out_specs = P("dp", "ctx", None)
    return jax.shard_map(body, mesh=mesh, in_specs=in_specs, out_specs=out_specs, check_vma=False)
```

```python
import functools
import math

import jax
import jax.numpy as jnp
from jax import lax
from jax.experimental import pallas as pl
from jax.experimental.pallas import tpu as pltpu
from jax.sharding import PartitionSpec as P

HEAD_TOTAL = 12
EPSILON = 1e-05
F32 = jnp.float32
BF16 = jnp.bfloat16
NT = (((1,), (1,)), ((), ()))
MIB = 1024 * 1024


def dot(a, b):
    return jnp.dot(a, b, preferred_element_type=F32)


def iota(shape, dim):
    return lax.broadcasted_iota(jnp.int32, shape, dim)


def embed_kernel(ctx, steps, split, x_hbm, w_hbm, *refs):
    slides, _, sub, width = x_hbm.shape
    outs, (early, late, weight, made, arrived, sent) = refs[:-6], refs[-6:]
    part = width // steps
    half = slides // 2
    loads = []
    for step in range(steps):
        columns = pl.ds(step * part, part)
        loads.append(
            (
                pltpu.make_async_copy(w_hbm.at[columns], weight.at[columns], arrived.at[0, step]),
                pltpu.make_async_copy(x_hbm.at[pl.ds(0, half), 0, :, columns], early.at[step], arrived.at[1, step]),
            )
        )
        for load in loads[-1]:
            load.start()
    last = pltpu.make_async_copy(x_hbm.at[pl.ds(half, slides - half), 0], late, arrived.at[0, steps])
    last.start()
    total = None
    for step in range(steps):
        for load in loads[step]:
            load.wait()
        product = dot(early[step].reshape(half * sub, part), weight[step * part : (step + 1) * part, :])
        total = product if total is None else total + product
    last.wait()
    totals = (total, dot(late[...].reshape((slides - half) * sub, width), weight[...]))
    me = lax.axis_index("dp")
    each = sub // ctx
    target, source = iota((sub, sub), 0), iota((sub, sub), 1)
    order = (source == target % each * ctx + target // each).astype(BF16)
    stores = []
    for slide in range(slides):
        start = slide % half * sub
        hidden = totals[slide // half][start : start + sub].astype(BF16).astype(F32)
        centered = hidden - jnp.mean(hidden, axis=-1, keepdims=True)
        variance = jnp.mean(centered * centered, axis=-1, keepdims=True)
        normed = (centered * lax.rsqrt(variance + EPSILON)).astype(BF16)
        made[slide] = dot(order, normed).astype(BF16).reshape(made.shape[1:])
        if split:
            stores.append(pltpu.make_async_copy(made.at[slide], outs[0].at[:, slide], sent.at[1, slide]))
            stores[-1].start()
    if not split:
        for other in range(slides):
            stores.append(pltpu.make_async_copy(made.at[me ^ other], outs[other], sent.at[0, other]))
            stores[-1].start()
    for store in stores:
        store.wait()


def part_kernel(by_residue, *outs):
    me = lax.axis_index("dp")
    for other, out in enumerate(outs):
        out[...] = by_residue[:, me ^ other]


def part_slides(by_residue):
    ctx, slides, each, features = by_residue.shape
    vmem = pl.BlockSpec(memory_space=pltpu.VMEM)
    return pl.pallas_call(
        part_kernel,
        out_shape=[jax.ShapeDtypeStruct((ctx, each, features), BF16)] * slides,
        in_specs=[vmem],
        out_specs=[vmem] * slides,
        compiler_params=pltpu.CompilerParams(vmem_limit_bytes=16 * MIB),
        cost_estimate=pl.CostEstimate(flops=10**6, bytes_accessed=10**4, transcendentals=0),
        name="part",
    )(by_residue)


def embed(tile_embed, w_in, ctx, split):
    slides, _, sub, width = tile_embed.shape
    features = w_in.shape[1]
    steps = 6
    part = width // steps
    shape = (ctx, sub // ctx, features) if split else (sub, features)
    if split:
        outs = [jax.ShapeDtypeStruct((ctx, slides, sub // ctx, features), BF16)]
    else:
        outs = [jax.ShapeDtypeStruct(shape, BF16)] * slides
    hbm = pl.BlockSpec(memory_space=pltpu.HBM)
    return pl.pallas_call(
        functools.partial(embed_kernel, ctx, steps, int(split)),
        out_shape=outs,
        in_specs=[hbm] * 2,
        out_specs=[hbm] * len(outs),
        scratch_shapes=[
            pltpu.VMEM((steps, slides // 2, sub, part), BF16),
            pltpu.VMEM((slides - slides // 2, sub, width), BF16),
            pltpu.VMEM((width, features), BF16),
            pltpu.VMEM((slides,) + shape, BF16),
            pltpu.SemaphoreType.DMA((2, steps + 1)),
            pltpu.SemaphoreType.DMA((2, slides)),
        ],
        compiler_params=pltpu.CompilerParams(vmem_limit_bytes=60 * MIB),
        name="embed",
    )(tile_embed, w_in)


def fetch_kernel(source, after, kept, ready):
    copy = pltpu.make_async_copy(source, kept, ready)
    copy.start()
    copy.wait()


def fetch(value, after):
    hbm = pl.BlockSpec(memory_space=pltpu.HBM)
    return pl.pallas_call(
        fetch_kernel,
        out_shape=jax.ShapeDtypeStruct(value.shape, value.dtype),
        in_specs=[hbm] * 2,
        out_specs=pl.BlockSpec(memory_space=pltpu.VMEM),
        scratch_shapes=[pltpu.SemaphoreType.DMA],
        compiler_params=pltpu.CompilerParams(vmem_limit_bytes=50 * MIB),
        cost_estimate=pl.CostEstimate(flops=0, bytes_accessed=8 * 10**6, transcendentals=0),
        name="fetch",
    )(value, after)


def project(rows, weight_ref, is_valid, keys, values):
    features = weight_ref.shape[0]
    made = dot(rows, weight_ref[:, features : 2 * features])
    keys[...] = jnp.where(is_valid, made, made[0:1]).astype(BF16)
    made = dot(rows, weight_ref[:, 2 * features :])
    values[...] = jnp.where(is_valid, made, 0.0).astype(BF16)


def queries_of(rows, weight_ref):
    features = weight_ref.shape[0]
    scale = math.log2(math.e) / math.sqrt(features // HEAD_TOTAL)
    return (dot(rows, weight_ref[:, :features]) * scale).astype(BF16)


def attend(queries, keys, values, counted, put, put_total):
    count, features = queries.shape
    width = features // HEAD_TOTAL
    pair = 2 * width
    even = iota((1, pair), 1) < width
    lane = iota((1, 128), 1)
    logs = jnp.zeros((count, 128), F32)
    for at in range(0, features, pair):
        columns = slice(at, at + pair)
        both = queries[:, columns]
        key_pair = keys[:, columns]
        value_pair = jnp.concatenate([values[:, columns], counted], axis=1)
        outs = []
        for side in range(2):
            mine = even if side == 0 else ~even
            scores = lax.dot_general(jnp.where(mine, both, 0).astype(BF16), key_pair, NT, preferred_element_type=F32)
            top = jnp.max(scores, axis=-1, keepdims=True)
            weights = jnp.exp2(scores - top).astype(BF16)
            summed = dot(weights, value_pair)
            outs.append(summed)
            logs = jnp.where(lane == at // width + side, top + jnp.log2(summed[:, pair : pair + 128]), logs)
        total = jnp.where(even, outs[0][:, pair:], outs[1][:, pair:])
        out = jnp.where(even, outs[0][:, :pair], outs[1][:, :pair])
        put(columns, (out / jnp.where(total > 0, total, 1.0)).astype(BF16))
    put_total(logs)


def local_kernel(dp, ctx, block, counts_ref, *refs):
    pieces, (weight_ref, out_ref, log_ref, rows, keys, values) = refs[:dp], refs[dp:]
    me = lax.axis_index("dp")
    sub = pieces[0].shape[0]
    for other, piece in enumerate(pieces):
        rows[pl.ds(pl.multiple_of((me ^ other) * sub, sub), sub), :] = piece[...]
    count = rows.shape[0]
    each = sub // ctx
    spot = iota((count, 1), 0)
    inner = spot % sub
    position = lax.axis_index("ctx") * count + spot // sub * sub + inner % each * ctx + inner // each
    is_valid = position < counts_ref[me]
    project(rows[...], weight_ref, is_valid, keys, values)
    counted = jnp.broadcast_to(is_valid.astype(F32), (count, 128)).astype(BF16)
    for start in range(0, count, block):

        def put(columns, out):
            out_ref[start : start + block, columns] = out

        def put_total(logs):
            log_ref[start : start + block, :] = logs

        attend(queries_of(rows[start : start + block, :], weight_ref), keys, values, counted, put, put_total)


def local_attention(tile_counts, pieces, w_qkv, ctx):
    dp = len(pieces)
    sub, features = pieces[0].shape
    count = dp * sub
    vmem = pl.BlockSpec(memory_space=pltpu.VMEM)
    return pl.pallas_call(
        functools.partial(local_kernel, dp, ctx, min(256, count)),
        out_shape=[jax.ShapeDtypeStruct((count, features), BF16), jax.ShapeDtypeStruct((count, 128), F32)],
        in_specs=[pl.BlockSpec(memory_space=pltpu.SMEM)] + [vmem] * (dp + 1),
        out_specs=[vmem] * 2,
        scratch_shapes=[pltpu.VMEM((count, features), BF16)] * 3,
        compiler_params=pltpu.CompilerParams(vmem_limit_bytes=24 * MIB),
        cost_estimate=pl.CostEstimate(flops=8 * 10**9, bytes_accessed=10**7, transcendentals=0),
        name="local",
    )(tile_counts, *pieces, w_qkv)


def packed_rows(portion, features):
    return portion * (features // 128) + 16


def dilated_kernel(dp, ctx, block, sends, counts_ref, rows, weight_ref, *refs):
    out_refs, (keys, values) = refs[:-2], refs[-2:]
    out_refs = [ref.at[place] for ref, group in zip(out_refs, sends) for place in range(len(group))]
    sends = [other for group in sends for other in group]
    me, mine = lax.axis_index("dp"), lax.axis_index("ctx")
    count, features = rows.shape
    portion = count // ctx
    each = portion // dp
    spot = iota((count, 1), 0)
    inner = spot % portion
    position = spot // portion * count + inner // each * (count // dp) + inner % each * ctx + mine
    is_valid = position < counts_ref[me]
    counted = jnp.broadcast_to(is_valid.astype(F32), (count, 128)).astype(BF16)
    project(rows[...], weight_ref, is_valid, keys, values)
    portions = block // portion
    for start in range(0, len(sends), portions):
        some = sends[start : start + portions]
        wanted = []
        for other in some:
            at = pl.multiple_of((mine ^ other) * portion, portion)
            wanted.append(rows[pl.ds(at, portion), :])

        def spread(columns, out):
            for place in range(len(some)):
                first = columns.start // 128 * portion
                out_refs[start + place][first : first + portion, :] = out[place * portion : (place + 1) * portion]

        def put_total(logs):
            high = logs.astype(BF16).astype(F32)
            low = logs - high
            lane = iota((1, 128), 1)
            both = jnp.where(lane < 16, high, pltpu.roll(low, 16, 1))
            both = jnp.where(lane < 32, both, 0.0)
            for place in range(len(some)):
                merged = both[place * portion : place * portion + 16]
                for group in range(1, portion // 16):
                    at = place * portion + group * 16
                    merged = merged + pltpu.roll(both[at : at + 16], 32 * group, 1)
                out_refs[start + place][-16:, :] = merged.astype(BF16)

        attend(queries_of(jnp.concatenate(wanted, axis=0), weight_ref), keys, values, counted, spread, put_total)


def dilated_attention(tile_counts, rows, w_qkv, dp, ctx, sends):
    count, features = rows.shape
    portion = count // ctx
    vmem = pl.BlockSpec(memory_space=pltpu.VMEM)
    return pl.pallas_call(
        functools.partial(dilated_kernel, dp, ctx, min(256, count), sends),
        out_shape=[jax.ShapeDtypeStruct((len(group), packed_rows(portion, features), 128), BF16) for group in sends],
        in_specs=[pl.BlockSpec(memory_space=pltpu.SMEM)] + [vmem] * 2,
        out_specs=[vmem] * len(sends),
        scratch_shapes=[pltpu.VMEM((count, features), BF16)] * 2,
        compiler_params=pltpu.CompilerParams(vmem_limit_bytes=24 * MIB),
        cost_estimate=pl.CostEstimate(flops=10**6, bytes_accessed=10**4, transcendentals=0),
        name="dilated",
    )(tile_counts, rows, w_qkv)


def merge_rows(own, own_logs, features_of, logs, heads, weight):
    lane = iota((1, 128), 1)
    share = jnp.where(lane < HEAD_TOTAL, 1.0 / (1.0 + jnp.exp2(own_logs - logs)), 0.0)
    high = share.astype(BF16)
    low = (share - high.astype(F32)).astype(BF16)
    wide = dot(high, heads) + dot(low, heads)
    own = own.astype(F32)
    merged = own + wide * (features_of.astype(F32) - own)
    return dot(merged.astype(BF16), weight)


def heads_of(features):
    return (iota((128, features), 0) == iota((128, features), 1) // (features // HEAD_TOTAL)).astype(BF16)


def merge_kernel(dp, ctx, counts_ref, out_ref, log_ref, weight_ref, dilated, mixed_ref):
    me, mine = lax.axis_index("dp"), lax.axis_index("ctx")
    count, features = out_ref.shape
    sub = count // dp
    each = sub // ctx
    heads = heads_of(features)
    target, source = iota((sub, sub), 0), iota((sub, sub), 1)
    order = (target == source % each * ctx + source // each).astype(BF16)
    for part in range(dp):
        rows = slice(part * sub, (part + 1) * sub)
        logs = dilated[rows, features:].astype(F32)
        logs = logs + pltpu.roll(logs, 128 - 16, 1)
        mixed = merge_rows(out_ref[rows, :], log_ref[rows, :], dilated[rows, :features], logs, heads, weight_ref[...])
        inner = iota((sub, 1), 0)
        position = mine * count + part * sub + inner % each * ctx + inner // each
        mixed = jnp.where(position < counts_ref[me], mixed, 0.0)
        mixed_ref[0, rows, :] = dot(order, mixed.astype(BF16)).astype(BF16)


def merge(tile_counts, out, logs, w_out, received, dp, ctx):
    count, features = out.shape
    vmem = pl.BlockSpec(memory_space=pltpu.VMEM)
    return pl.pallas_call(
        functools.partial(merge_kernel, dp, ctx),
        out_shape=jax.ShapeDtypeStruct((1, count, features), BF16),
        in_specs=[pl.BlockSpec(memory_space=pltpu.SMEM)] + [vmem] * 4,
        out_specs=vmem,
        compiler_params=pltpu.CompilerParams(vmem_limit_bytes=24 * MIB),
        name="merge",
    )(tile_counts, out, logs, w_out, received)


def merge_part_kernel(dp, ctx, sends, with_others, counts_ref, out_ref, log_ref, weight_ref, *refs):
    pieces, refs = refs[: len(sends)], refs[len(sends) :]
    pieces = [(other, ref.at[place]) for ref, group in zip(pieces, sends) for place, other in enumerate(group)]
    sends = [other for other, _ in pieces]
    mixed_ref, (dilated, own, own_logs, ready, sent) = refs[-6], refs[-5:]
    me, mine = lax.axis_index("dp"), lax.axis_index("ctx")
    count, features = out_ref.shape
    sub = count // dp
    each = sub // ctx
    portion = count // ctx
    span = len(sends) * each
    first = (mine ^ sends[0]) // len(sends) * len(sends)
    for part in range(dp):
        at = pl.multiple_of(part * sub + first * each, each)
        own[part * span : (part + 1) * span, :] = out_ref[pl.ds(at, span), :]
        own_logs[part * span : (part + 1) * span, :] = log_ref[pl.ds(at, span), :]
    for other, piece in pieces:
        for part in range(dp):
            at = pl.multiple_of(part * span + ((mine ^ other) - first) * each, each)
            for block in range(features // 128):
                start = block * portion + part * each
                dilated[pl.ds(at, each), block * 128 : (block + 1) * 128] = piece[start : start + each, :]
            dilated[pl.ds(at, each), features:] = pltpu.roll(
                piece[-16:, :].astype(F32), (128 - 32 * part) % 128, 1
            ).astype(BF16)
    logs = dilated[:, features:].astype(F32)
    logs = logs + pltpu.roll(logs, 128 - 16, 1)
    mixed = merge_rows(own[...], own_logs[...], dilated[:, :features], logs, heads_of(features), weight_ref[...])
    spot = iota((dp * span, 1), 0)
    inner = spot % span
    position = mine * count + spot // span * sub + inner % each * ctx + first + inner // each
    mixed = jnp.where(position < counts_ref[me], mixed, 0.0).astype(BF16)
    target, source = iota((sub, span), 0), iota((sub, span), 1)
    order = (target == source % each * ctx + first + source // each).astype(BF16)
    stores = []
    for part in range(dp):
        made = dot(order, mixed[part * span : (part + 1) * span])
        rows = slice(part * sub, (part + 1) * sub)
        if with_others:
            ready[rows, :] = (made + refs[0][rows, :].astype(F32)).astype(BF16)
            stores.append(pltpu.make_async_copy(ready.at[rows], mixed_ref.at[0, rows], sent.at[part]))
            stores[-1].start()
        else:
            mixed_ref[rows, :] = made.astype(BF16)
    for store in stores:
        store.wait()


def merge_part(tile_counts, out, logs, w_out, received, dp, ctx, sends, others=()):
    count, features = out.shape
    vmem = pl.BlockSpec(memory_space=pltpu.VMEM)
    shape = (1, count, features) if others else (count, features)
    rows = count * sum(len(group) for group in sends) // ctx
    return pl.pallas_call(
        functools.partial(merge_part_kernel, dp, ctx, sends, len(others)),
        out_shape=jax.ShapeDtypeStruct(shape, BF16),
        in_specs=[pl.BlockSpec(memory_space=pltpu.SMEM)] + [vmem] * (3 + len(received) + len(others)),
        out_specs=pl.BlockSpec(memory_space=pltpu.HBM) if others else vmem,
        scratch_shapes=[
            pltpu.VMEM((rows, features + 128), BF16),
            pltpu.VMEM((rows, features), BF16),
            pltpu.VMEM((rows, 128), F32),
            pltpu.VMEM((count if others else 16, features), BF16),
            pltpu.SemaphoreType.DMA((dp,)),
        ],
        compiler_params=pltpu.CompilerParams(vmem_limit_bytes=24 * MIB),
        cost_estimate=pl.CostEstimate(flops=10**6, bytes_accessed=10**4, transcendentals=0),
        name="merge",
    )(tile_counts, out, logs, w_out, *received, *others)


def exchange(value, axis, other):
    if other == 0:
        return value
    return lax.ppermute(value, axis, [(i, i ^ other) for i in range(lax.axis_size(axis))])


def body(tile_embed, tile_counts, w_in, w_qkv, w_out):
    dp, ctx = lax.axis_size("dp"), lax.axis_size("ctx")
    slides, _, sub, _ = tile_embed.shape
    features = w_out.shape[0]
    count = sub * dp
    each = sub // ctx
    aligned = each % 16 == 0 and ctx <= 8
    made = embed(tile_embed, w_in, ctx, aligned)
    if aligned:
        by_residue, made = made[0], part_slides(made[0])
    else:
        slide_of = [lax.axis_index("dp") ^ other for other in range(dp)]
        stacked = jnp.stack(made)[jnp.stack(slide_of)]
        by_residue = stacked.reshape(slides, ctx, each, features).swapaxes(0, 1)
    pieces = [exchange(piece, "dp", other).reshape(sub, features) for other, piece in enumerate(made)]
    regrouped = lax.all_to_all(
        by_residue.reshape(ctx * dp, each, features), ("ctx", "dp"), split_axis=0, concat_axis=0, tiled=True
    ).reshape(count, features)
    regrouped, *pieces = lax.optimization_barrier((regrouped, *pieces))
    w_near = fetch(w_qkv, made[0])
    portion = count // ctx
    if aligned:
        if ctx == 8:
            far, sends = ((5,), (4,), (7,), (6,)), ((2, 3), (1,), (0,))
            *across, two_three, one, own = dilated_attention(tile_counts, regrouped, w_near, dp, ctx, far + sends)
            across = [exchange(piece, "ctx", other) for piece, (other,) in zip(across, far)]
            two_three = exchange(two_three, "ctx", 2)
            one_three = exchange(jnp.concatenate([one, two_three[1:]]), "ctx", 1)
            parts = [((2,), (0,), (1, 3)), [two_three, own, one_three]], [far, across]
        else:
            sends = tuple((other,) for other in range(ctx))
            own, *made = dilated_attention(tile_counts, regrouped, w_near, dp, ctx, sends)
            made = [exchange(piece, "ctx", other) for piece, (other,) in zip(made, sends[1:])]
            parts = ([sends, [own, *made]],)
        own, *pieces = lax.optimization_barrier((own, *pieces))
        parts[0][1][1 if ctx == 8 else 0] = own
        out, logs = local_attention(tile_counts, pieces, w_near, ctx)
        mixed = ()
        for sends, received in parts:
            mixed = (merge_part(tile_counts, out, logs, w_out, received, dp, ctx, sends, mixed),)
        return mixed[0].reshape(1, count, features)
    else:
        out, logs = local_attention(tile_counts, pieces, w_near, ctx)
        made = dilated_attention(tile_counts, regrouped, w_near, dp, ctx, (tuple(range(ctx)),))[0]
        order = jnp.stack([lax.axis_index("ctx") ^ other for other in range(ctx)])
        packed = lax.all_to_all(made[order], "ctx", split_axis=0, concat_axis=0, tiled=True)
        wide = packed[:, :-16].reshape(ctx, features // 128, portion, 128).swapaxes(1, 2).reshape(ctx, portion, features)
        lanes = packed[:, -16:].reshape(ctx, 16, 4, 32).swapaxes(1, 2)[:, : portion // 16].reshape(ctx, portion, 32)
        whole = jnp.concatenate([wide, jnp.pad(lanes, ((0, 0), (0, 0), (0, 96)))], axis=-1)
        received = whole.reshape(ctx, dp, each, -1).swapaxes(0, 1).reshape(count, -1)
        return merge(tile_counts, out, logs, w_out, received, dp, ctx)


def solution(mesh):
    in_specs = (P(None, "ctx", "dp", None), P(), P(), P(), P())
    out_specs = P("dp", "ctx", None)
    return jax.shard_map(body, mesh=mesh, in_specs=in_specs, out_specs=out_specs, check_vma=False)
```
